512 devices in a mesh: dp: 8 (over z), cells: 64 (over y, x, core).
Axes of the slice: x: 4, y: 8, z: 8, core: 2. Of those that a mesh axis runs over, the one named last changes fastest.
Arguments:
- vectors: bfloat16 [262144, 768], P(('dp', 'cells')), may hold values from -7 to 7
- cell_of: int32 [262144], P(('dp', 'cells')), may hold values from 0 to 2047, as said below
- cell_slot: int32 [2048], replicated, may hold values from 0 to 2047, as said below
- coarse: bfloat16 [2048, 768], P('cells'), may hold values from -6 to 6
- fine_book: bfloat16 [2048, 256, 768], P(('dp', 'cells')), may hold values from -8.375 to 8.375
Outputs:
- coarse_share: float32 [2048], replicated
- fine_next: bfloat16 [2048, 256, 768], P(('dp', 'cells'))
- distortion: float32 [262144], P(('dp', 'cells'))
The draws below stay inside these ranges and needn't reach their ends.
Inputs may be any that keep to these rules, and one draw needn't show every extreme that they name: `cell_slot`: A permutation: every slot holds exactly one cell. The slots s with s // 4 = g lie on the device of flat index g over dp then cells. `cell_of`: every vector's slot lies on a device of the vector's own dp index. Of the vectors of one device, at most 16 have slots on any one device, and some devices receive exactly 16 from every device of their dp index.
All inputs are finite; a program needn't handle non-finite values.
Results may differ from the reference program's by a relative error of at most 0.0026.
Values may be sent and summed in bfloat16 or wider, within the bound.
No kernel may reach another device: no remote copies, remote signals or barrier semaphores. Data moves between devices by JAX's collectives and lax.ppermute only.
A program may use at most 64 MiB of HBM per device.

```python
import jax
import jax.numpy as jnp
from jax import lax

D = 768
FINE = 256
CELL_OWN = 4
ROWS = 512
COARSE = 2048
VECTORS = 262144
CAP = 16
N_DP = 8
N_CELLS = 64
DEVICES = 512


def slot_table(key):
    return jax.random.permutation(key, COARSE).astype(jnp.int32)


def draw_cell_slot(key, part):
    return slot_table(key)


def draw_vectors(key, part):
    key = jax.random.fold_in(key, 1)
    base_key = jax.random.fold_in(key, 0)
    values = jnp.clip(jax.random.normal(base_key, (VECTORS, D), jnp.float32), -6.0, 6.0)
    return values.astype(jnp.bfloat16)


def draw_cell_of(key, part):
    slot_of_cell = slot_table(key)
    key = jax.random.fold_in(key, 3)
    cell_at_slot = jnp.argsort(slot_of_cell).astype(jnp.int32)
    hot_key, device_key = jax.random.split(key)

    def row_order(row_key):
        return jax.random.permutation(row_key, N_CELLS).astype(jnp.int32)
    ranks_row = jax.vmap(row_order)(jax.random.split(hot_key, N_DP))
    hot_table = (ranks_row < N_CELLS // 8).astype(jnp.int32)
    top_owners = 3 * N_CELLS // 8
    half_cap = CAP // 2
    place = jnp.arange(ROWS, dtype=jnp.int32)
    rank_of_row = jnp.where(place < top_owners * CAP, place // CAP, top_owners + (place - top_owners * CAP) // half_cap)

    def one_device(device, dev_key):
        row_index = device // N_CELLS
        order_key, cell_key, mix_key = jax.random.split(dev_key, 3)
        score = hot_table[row_index] * N_CELLS + jax.random.permutation(order_key, N_CELLS).astype(jnp.int32)
        ranking = jnp.argsort(-score).astype(jnp.int32)
        column = ranking[rank_of_row]
        local = jax.random.randint(cell_key, (ROWS,), 0, CELL_OWN, dtype=jnp.int32)
        slot = (row_index * N_CELLS + column) * CELL_OWN + local
        chosen = cell_at_slot[slot]
        return chosen[jax.random.permutation(mix_key, ROWS)]
    devices_all = jnp.arange(DEVICES, dtype=jnp.int32)
    every = jax.vmap(one_device)(devices_all, jax.random.split(device_key, DEVICES))
    return every.reshape(VECTORS).astype(jnp.int32)


def steps_of(key, extent, pieces, smallest, top_value):
    loudness, own = 1.0, jax.random.fold_in(key, 6)
    for axis_at, parts in pieces:
        heights = jnp.exp(jax.random.uniform(jax.random.fold_in(own, axis_at), (parts,), jnp.float32, smallest / len(pieces), top_value / len(pieces)))
        loudness = loudness * jnp.repeat(heights, extent[axis_at] // parts).reshape([-1 if axis == axis_at else 1 for axis in range(len(extent))])
    return loudness


def normal_values(rng, shape, scale, bound, pieces=(), kind=jnp.bfloat16):
    gain = steps_of(rng, shape, pieces, -0.22, 0.18) if pieces else 1.0
    drawn = jax.random.normal(rng, shape, jnp.float32) * scale * gain
    return jnp.minimum(jnp.maximum(drawn, -bound), bound).astype(kind)


def setup_inputs(seed: int = 0) -> dict:
    key_list = jax.random.split(jax.random.key(seed), 6)
    return {
        "vectors": draw_vectors(jax.random.fold_in(key_list[5], 71), 0),
        "cell_of": draw_cell_of(jax.random.fold_in(key_list[5], 71), 0),
        "cell_slot": draw_cell_slot(jax.random.fold_in(key_list[5], 71), 0),
        "coarse": normal_values(key_list[3], (COARSE, D), 1.0, 6.0, ((0, 64),)),
        "fine_book": normal_values(key_list[4], (COARSE, FINE, D), 1.4, 8.375, ((0, 512),)),
    }


sharpness = 0.0625


def distance_block(points, point_squares, centres):
    wide = centres.astype(jnp.float32)
    centre_squares = jnp.sum(wide * wide, axis=1)
    products = lax.dot_general(points, centres, (((1,), (1,)), ((), ())), preferred_element_type=jnp.float32)
    return point_squares[:, None] + centre_squares[None, :] - 2.0 * products


def fine_owner(residual, local_cell, book):
    cells_here, fine_count, feature_count = book.shape
    flat_book = book.reshape(cells_here * fine_count, feature_count)
    present = (local_cell >= 0).astype(jnp.float32)
    chosen = jnp.maximum(local_cell, 0)
    residual_wide = residual.astype(jnp.float32)
    distance = distance_block(residual, jnp.sum(residual_wide * residual_wide, axis=1), flat_book)
    column_cell = jnp.arange(cells_here * fine_count, dtype=jnp.int32) // fine_count
    inside = column_cell[None, :] == chosen[:, None]
    scores = jnp.where(inside, -sharpness * distance, -jnp.inf)
    weights = jax.nn.softmax(scores, axis=1) * present[:, None]
    spread = jnp.sum(jnp.where(inside, weights * distance, 0.0), axis=1) / feature_count
    fine_mass = jnp.sum(weights, axis=0)
    totals = lax.dot_general(weights.astype(jnp.bfloat16), residual, (((0,), (0,)), ((), ())), preferred_element_type=jnp.float32)
    updated = (flat_book.astype(jnp.float32) + totals) / (1.0 + fine_mass[:, None])
    return spread, updated.astype(jnp.bfloat16).reshape(book.shape)


def reference(vectors, cell_of, cell_slot, coarse, fine_book):
    total_rows, feature_count = vectors.shape
    slot_count = coarse.shape[0]
    owners = slot_count // CELL_OWN
    window = CAP * N_CELLS

    def coarse_block(total, block):
        wide = block.astype(jnp.float32)
        distance = distance_block(block, jnp.sum(wide * wide, axis=1), coarse)
        probs = jax.nn.softmax(-sharpness * distance, axis=1)
        return total + jnp.sum(probs, axis=0), jnp.zeros((), jnp.float32)

    occupancy, unused = lax.scan(coarse_block, jnp.zeros((slot_count,), jnp.float32), vectors.reshape(-1, 512, feature_count))
    coarse_share = occupancy * (slot_count / total_rows)

    residual = (vectors.astype(jnp.float32) - coarse[cell_of].astype(jnp.float32)).astype(jnp.bfloat16)
    slot = cell_slot[cell_of]
    owner = (slot // CELL_OWN).astype(jnp.int32)
    local = (slot % CELL_OWN).astype(jnp.int32)
    order = jnp.argsort(owner, stable=True).astype(jnp.int32)
    counts = jax.ops.segment_sum(jnp.ones((total_rows,), jnp.int32), owner, num_segments=owners).astype(jnp.int32)
    starts = (jnp.cumsum(counts) - counts).astype(jnp.int32)
    padded_rows = jnp.concatenate([residual[order], jnp.zeros((window, feature_count), jnp.bfloat16)], axis=0)
    padded_cells = jnp.concatenate([local[order], jnp.full((window,), -1, jnp.int32)], axis=0)

    def one_owner(owner_id):
        begin = starts[owner_id]
        block_rows = lax.dynamic_slice_in_dim(padded_rows, begin, window, 0)
        block_cells = lax.dynamic_slice_in_dim(padded_cells, begin, window, 0)
        live = jnp.arange(window, dtype=jnp.int32) < counts[owner_id]
        block_cells = jnp.where(live, block_cells, -1).astype(jnp.int32)
        book = lax.dynamic_slice_in_dim(fine_book, (owner_id * CELL_OWN).astype(jnp.int32), CELL_OWN, 0)
        return fine_owner(block_rows, block_cells, book)

    spreads, books = lax.map(one_owner, jnp.arange(owners, dtype=jnp.int32))
    fine_next = books.reshape(fine_book.shape)
    sorted_owner = owner[order]
    rank = (jnp.arange(total_rows, dtype=jnp.int32) - starts[sorted_owner]).astype(jnp.int32)
    values = spreads[sorted_owner, rank]
    distortion = jnp.zeros((total_rows,), jnp.float32).at[order].set(values)
    return coarse_share, fine_next, distortion
```

```python
import functools

import jax
import jax.numpy as jnp
from jax import lax
from jax.experimental import pallas as pl
from jax.experimental.pallas import tpu as pltpu
from jax.sharding import Mesh, PartitionSpec as P

sharpness = 0.0625
Z, Y, X, CORES = 8, 8, 4, 2
PLANE = ("y", "x", "c")
EVERY = ("z", "y", "x", "c")
SETS = 4
f32, bf16, i32 = jnp.float32, jnp.bfloat16, jnp.int32
VMEM = pl.BlockSpec(memory_space=pltpu.VMEM)
SMEM = pl.BlockSpec(memory_space=pltpu.SMEM)


def params(cost):
    return dict(
        compiler_params=pltpu.CompilerParams(vmem_limit_bytes=48 * 2**20),
        cost_estimate=pl.CostEstimate(flops=cost, bytes_accessed=4 * 2**20, transcendentals=0),
    )


def iota(shape, axis):
    return lax.broadcasted_iota(i32, shape, axis)


def dot(a, b, ca, cb, precision=None):
    return lax.dot_general(
        a, b, (((ca,), (cb,)), ((), ())), preferred_element_type=f32, precision=precision
    )


def as_row(column):
    return jnp.transpose(jnp.broadcast_to(column, (column.shape[0], 128)))[0:1, :]


def route_kernel(owned, cell, table, vectors, send, meta, place):
    owners, cap, _ = send.shape
    rows = vectors.shape[0]
    high, low = table.shape
    cell_of = cell[...]
    slots = table[...]
    in_high = (iota((high, rows), 0) == cell_of // low).astype(bf16)
    in_low = iota((low, rows), 0) == cell_of % low
    owner_table = ((slots // owned) % owners).astype(bf16)
    local_table = (slots % owned).astype(bf16)
    owner = jnp.sum(jnp.where(in_low, dot(owner_table, in_high, 0, 0), 0.0), axis=0, keepdims=True)
    local = jnp.sum(jnp.where(in_low, dot(local_table, in_high, 0, 0), 0.0), axis=0, keepdims=True)
    at_owner = iota((owners, rows), 0) == owner.astype(i32)
    before = (iota((rows, rows), 0) < iota((rows, rows), 1)).astype(bf16)
    earlier = dot(at_owner.astype(bf16), before, 1, 0)
    rank = jnp.sum(jnp.where(at_owner, earlier, 0.0), axis=0, keepdims=True).astype(i32)
    position = owner.astype(i32) * cap + rank
    place[...] = position
    at_rank = (iota((cap, rows), 0) == rank).astype(bf16)
    found = dot(jnp.where(at_owner, local + 1.0, 0.0).astype(bf16), at_rank, 1, 1) - 1.0
    meta[...] = found.reshape(owners, 1, cap)
    block = 256
    for b in range(owners * cap // block):
        pick = (iota((block, rows), 0) + b * block == position).astype(bf16)
        moved = dot(pick, vectors[...], 1, 0).astype(bf16)
        send[b * block // cap : (b + 1) * block // cap] = moved.reshape(block // cap, cap, -1)


def route(vectors, cell_of, cell_slot, owners, cap, owned):
    rows, features = vectors.shape
    return pl.pallas_call(
        functools.partial(route_kernel, owned),
        out_shape=(
            jax.ShapeDtypeStruct((owners, cap, features), bf16),
            jax.ShapeDtypeStruct((owners, 1, cap), f32),
            jax.ShapeDtypeStruct((1, rows), i32),
        ),
        in_specs=[VMEM] * 3,
        out_specs=(VMEM,) * 3,
        name="route",
        **params(2 * 10**9),
    )(cell_of.reshape(1, rows), cell_slot.reshape(-1, 64), vectors)


def squares_kernel(book, vectors, book_squares, vector_squares):
    block = 256
    for b in range(book.shape[0] // block):
        at = slice(b * block, (b + 1) * block)
        wide = book[at].astype(f32)
        book_squares[at] = jnp.sum(wide * wide, axis=1, keepdims=True)
    for b in range(vectors.shape[0] // block):
        at = slice(b * block, (b + 1) * block)
        wide = vectors[at].astype(f32)
        vector_squares[:, at] = as_row(jnp.sum(wide * wide, axis=1, keepdims=True))


def squares(book, vectors):
    return pl.pallas_call(
        squares_kernel,
        out_shape=(
            jax.ShapeDtypeStruct((book.shape[0], 1), f32),
            jax.ShapeDtypeStruct((1, vectors.shape[0]), f32),
        ),
        in_specs=[VMEM] * 2,
        out_specs=(VMEM,) * 2,
        name="squares",
        **params(10**9),
    )(book, vectors)


def coarse_kernel(
    where, vectors, vector_squares, slots, own, right, left, far_a, far_b, own2, right2, left2, far_a2, far_b2,
    share, mine, scores,
):
    base, quarter, core = where[0], where[1], where[2]
    rows = vectors.shape[0]
    groups = scores.shape[0]
    picked = jnp.zeros((8, vectors.shape[1]), f32)
    top = jnp.full((1, rows), -jnp.inf, f32)
    half = groups // 2
    for side, chunks in ((core, (own, right, left, far_a, far_b)), (1 - core, (own2, right2, left2, far_a2, far_b2))):
        for chunk, step, start in zip(chunks, (0, 1, 3, 2, 2), (0, 0, 0, 0, half), strict=True):
            count = chunk.shape[0] // 8
            at = side * SETS + (quarter + step) % SETS
            points = chunk[...]
            wide = points.astype(f32)
            distance = (
                vector_squares[...] + jnp.sum(wide * wide, axis=1, keepdims=True) - 2.0 * dot(points, vectors[...], 1, 1)
            )
            score = -sharpness * distance
            top = jnp.maximum(top, jnp.max(score, axis=0, keepdims=True))
            scores[start : start + count, at] = score.reshape(count, 8, rows)
            held = slots[at][:, start * 8 : (start + count) * 8]
            inside = (iota((8, count * 8), 0) + base == held) & (iota((8, count * 8), 0) < SETS)
            picked = picked + dot(inside.astype(bf16), points, 1, 0)
    mine[...] = picked.astype(bf16)
    total = jnp.zeros((1, rows), f32)
    blocks = groups // 2
    for b in range(blocks):
        e = jnp.exp(scores[2 * b : 2 * b + 2].reshape(128, rows) - top)
        total = total + jnp.sum(e, axis=0, keepdims=True)
        scores[2 * b : 2 * b + 2] = e.reshape(2, 8, 8, rows)
    inverse = 1.0 / total
    for b in range(blocks):
        probs = scores[2 * b : 2 * b + 2].reshape(128, rows) * inverse
        lanes = probs[:, 0:128]
        for j in range(1, rows // 128):
            lanes = lanes + probs[:, j * 128 : (j + 1) * 128]
        share[b : b + 1, :] = jnp.sum(jnp.transpose(lanes), axis=0, keepdims=True)


def coarse_part(where, vectors, vector_squares, slots, chunks):
    rows, features = vectors.shape
    groups = Y * X
    return pl.pallas_call(
        coarse_kernel,
        out_shape=(
            jax.ShapeDtypeStruct((groups // 2, 128), f32),
            jax.ShapeDtypeStruct((8, features), bf16),
        ),
        in_specs=[SMEM] + [VMEM] * (3 + len(chunks)),
        out_specs=(VMEM,) * 2,
        scratch_shapes=[pltpu.VMEM((groups, CORES * SETS, 8, rows), f32)],
        name="coarse_part",
        **params(2 * 10**9),
    )(where, vectors, vector_squares, slots, *chunks)


def fine_kernel(got, meta, mine, book, book_squares, spread, weights, residual, mass):
    owners, _, cap = meta.shape
    rows, features = got.shape
    count = book.shape[0]
    fine = count // SETS
    spread_places = (iota((cap, rows), 1) % cap == iota((cap, rows), 0)).astype(bf16)
    at_owner = iota((owners, rows), 1) // cap == iota((owners, rows), 0)
    across = dot(meta[...].reshape(owners, cap).astype(bf16), spread_places, 1, 0)
    local = jnp.sum(jnp.where(at_owner, across, 0.0), axis=0, keepdims=True)
    block = 256
    parts = []
    for b in range(rows // block):
        at = slice(b * block, (b + 1) * block)
        slot = local[:, at]
        inside = [slot == s for s in range(SETS)]
        chosen = (iota((8, block), 0).astype(f32) == slot).astype(bf16)
        base = dot(chosen, mine[...], 0, 0)
        moved = (got[at].astype(f32) - base).astype(bf16)
        residual[at] = moved
        wide = moved.astype(f32)
        moved_squares = as_row(jnp.sum(wide * wide, axis=1, keepdims=True))
        distance = jnp.zeros((fine, block), f32)
        for s in range(SETS):
            of = slice(s * fine, (s + 1) * fine)
            here = moved_squares + book_squares[of] - 2.0 * dot(book[of], moved, 1, 1)
            distance = jnp.where(inside[s], here, distance)
        score = -sharpness * distance
        e = jnp.exp(score - jnp.max(score, axis=0, keepdims=True))
        weight = e * ((slot >= 0.0).astype(f32) / jnp.sum(e, axis=0, keepdims=True))
        parts.append(jnp.sum(weight * distance, axis=0, keepdims=True) / features)
        for s in range(SETS):
            of = slice(s * fine, (s + 1) * fine)
            only = jnp.where(inside[s], weight, 0.0)
            weights[of, at] = only.astype(bf16)
            part = jnp.sum(only, axis=1, keepdims=True)
            mass[of] = part if b == 0 else mass[of] + part
    row = jnp.concatenate(parts, axis=1)
    spread[...] = dot(
        jnp.where(at_owner, row, 0.0), spread_places.astype(f32), 1, 1, lax.Precision.HIGHEST
    ).reshape(owners, 1, cap)


def fine_part(got, meta, mine, book, book_squares):
    owners, _, cap = meta.shape
    rows, features = got.shape
    count = book.shape[0]
    return pl.pallas_call(
        fine_kernel,
        out_shape=(
            jax.ShapeDtypeStruct((owners, 1, cap), f32),
            jax.ShapeDtypeStruct((count, rows), bf16),
            jax.ShapeDtypeStruct((rows, features), bf16),
            jax.ShapeDtypeStruct((count, 1), f32),
        ),
        in_specs=[VMEM] * 5,
        out_specs=(VMEM,) * 4,
        name="fine_part",
        **params(3 * 10**9),
    )(got, meta, mine, book, book_squares)


def update_kernel(book, weights, residual, mass, out):
    block = 256
    for b in range(book.shape[0] // block):
        at = slice(b * block, (b + 1) * block)
        total = dot(weights[at], residual[...], 1, 0)
        out[at] = ((book[at].astype(f32) + total) * (1.0 / (1.0 + mass[at]))).astype(bf16)


def update(book, weights, residual, mass):
    return pl.pallas_call(
        update_kernel,
        out_shape=jax.ShapeDtypeStruct(book.shape, bf16),
        in_specs=[VMEM] * 4,
        out_specs=VMEM,
        name="update",
        **params(3 * 10**9),
    )(book, weights, residual, mass)


def pick_kernel(returned, place, out):
    owners, _, cap = returned.shape
    rows = place.shape[1]
    position = place[...]
    at_owner = (iota((owners, rows), 0) == position // cap).astype(f32)
    at_rank = iota((cap, rows), 0) == position % cap
    across = dot(returned[...].reshape(owners, cap), at_owner, 0, 0, lax.Precision.HIGHEST)
    out[...] = jnp.sum(jnp.where(at_rank, across, 0.0), axis=0, keepdims=True)


def pick(returned, place):
    return pl.pallas_call(
        pick_kernel,
        out_shape=jax.ShapeDtypeStruct(place.shape, f32),
        in_specs=[VMEM] * 2,
        out_specs=VMEM,
        name="pick",
        **params(10**8),
    )(returned, place)


def exchange(x, axes):
    return lax.all_to_all(x, axes, 0, 0, tiled=True)


def add_over(x, axes, count):
    return jnp.sum(exchange(jnp.broadcast_to(x[None], (count, *x.shape)), axes), axis=0)


def gather_coarse(coarse, quarter):
    features = coarse.shape[1]
    rows = coarse.shape[0] // SETS
    part = lax.dynamic_slice_in_dim(coarse, quarter * rows, rows, 0)
    groups = Y * X
    own = exchange(jnp.broadcast_to(part[None], (groups, rows, features)), ("y", "x"))
    own = own.reshape(groups * rows, features)
    up = [(i, (i + 1) % Z) for i in range(Z)]
    down = [(i, (i - 1) % Z) for i in range(Z)]
    right = lax.ppermute(own, "z", down)
    left = lax.ppermute(own, "z", up)
    half = groups * rows // 2
    far_a = lax.ppermute(right[:half], "z", down)
    far_b = lax.ppermute(left[half:], "z", up)
    chunks = (own, right, left, far_a, far_b)
    return chunks + tuple(lax.ppermute(chunk, "c", [(0, 1), (1, 0)]) for chunk in chunks)


def on_device(vectors, cell_of, cell_slot, coarse, fine_book):
    rows, features = vectors.shape
    owned, fine, _ = fine_book.shape
    owners = Y * X * CORES
    cap = 2 * rows // owners
    cells = cell_slot.shape[0]
    z, c = lax.axis_index("z"), lax.axis_index("c")
    base = lax.axis_index(EVERY) * owned
    where = jnp.stack([base, z % SETS, c]).astype(i32)
    book = fine_book.reshape(owned * fine, features)

    send, meta, place = route(vectors, cell_of, cell_slot, owners, cap, owned)
    got = exchange(send, PLANE).reshape(owners * cap, features)
    got_meta = exchange(meta, PLANE)
    chunks = gather_coarse(coarse, z % SETS)
    book_squares, vector_squares = squares(book, vectors)
    slots = cell_slot.reshape(Y * X, CORES, SETS, 8).transpose(1, 2, 0, 3).reshape(CORES * SETS, 1, Y * X * 8)
    share, mine = coarse_part(where, vectors, vector_squares, slots, chunks)
    share = add_over(share, ("z", "c"), Z * CORES)
    share = add_over(share, ("y", "x"), Y * X)
    coarse_share = (share * (owned / rows)).reshape(cells)

    spread, weights, residual, mass = fine_part(got, got_meta, mine, book, book_squares)
    returned = exchange(spread, PLANE)
    fine_next = update(book, weights, residual, mass).reshape(fine_book.shape)
    distortion = pick(returned, place).reshape(rows)
    return (coarse_share, fine_next, distortion)


def solution(mesh):
    grid = Mesh(mesh.devices.reshape(Z, Y, X, CORES), EVERY)
    return jax.shard_map(
        on_device,
        mesh=grid,
        in_specs=(P(EVERY, None), P(EVERY), P(), P(PLANE, None), P(EVERY, None, None)),
        out_specs=(P(), P(EVERY, None, None), P(EVERY)),
        check_vma=False,
    )
```

```python
import functools

import jax
import jax.numpy as jnp
from jax import lax
from jax.experimental import pallas as pl
from jax.experimental.pallas import tpu as pltpu
from jax.sharding import Mesh, PartitionSpec as P

sharpness = 0.0625
Z, Y, X, CORES = 8, 8, 4, 2
PLANE = ("y", "x", "c")
EVERY = ("z", "y", "x", "c")
GROUPS = Y * X
SETS = 4
LOW = 64
f32, bf16, i32 = jnp.float32, jnp.bfloat16, jnp.int32
VMEM = pl.BlockSpec(memory_space=pltpu.VMEM)
SMEM = pl.BlockSpec(memory_space=pltpu.SMEM)


def call(body, out_shape, scalars, arrays, name, flops, mib=16, scratch=()):
    return pl.pallas_call(
        body,
        out_shape=out_shape,
        in_specs=[SMEM] * len(scalars) + [VMEM] * len(arrays),
        out_specs=jax.tree.map(lambda _: VMEM, out_shape),
        scratch_shapes=scratch,
        name=name,
        compiler_params=pltpu.CompilerParams(vmem_limit_bytes=mib * 2**20),
        cost_estimate=pl.CostEstimate(flops=flops, bytes_accessed=2**20, transcendentals=0),
    )(*scalars, *arrays)


def shaped(shape, dtype):
    return jax.ShapeDtypeStruct(shape, dtype)


def iota(shape, axis):
    return lax.broadcasted_iota(i32, shape, axis)


def dot(a, b, ca, cb, precision=None):
    return lax.dot_general(
        a, b, (((ca,), (cb,)), ((), ())), preferred_element_type=f32, precision=precision
    )


def as_row(column):
    return jnp.transpose(jnp.broadcast_to(column, (column.shape[0], 128)))[0:1, :]


def row_squares(points):
    wide = points.astype(f32)
    return jnp.sum(wide * wide, axis=1, keepdims=True)


def pack_kernel(where, coarse, cell, out):
    rows, features = coarse.shape
    wide = coarse[...].astype(f32).reshape(SETS, rows // SETS, features)
    part = jnp.sum(jnp.where(iota(wide.shape, 0) == where[1], wide, 0.0), axis=0)
    ids = jnp.concatenate([cell[...] // LOW, cell[...] % LOW], axis=0).astype(f32)
    out[...] = jnp.broadcast_to(jnp.concatenate([part, ids], axis=1).astype(bf16)[None], out.shape)


def split_kernel(got, own, own_a, own_b, ids):
    features = own.shape[1]
    whole = got[...].astype(f32)
    rows = whole[:, :, :features].reshape(own.shape).astype(bf16)
    half = own.shape[0] // 2
    own[...] = rows
    own_a[...] = rows[:half]
    own_b[...] = rows[half:]
    ids[...] = whole[:, :, features:]


def prepare_kernel(owned, where, cell, table, vectors, vectors2, book, send, place, book_squares, vector_squares, wanted):
    owners, cap, _ = send.shape
    rows = vectors.shape[0]
    high, low = table.shape
    cell_of = cell[...]
    slots = table[...]
    in_high = (iota((high, rows), 0) == cell_of // low).astype(bf16)
    in_low = iota((low, rows), 0) == cell_of % low
    owner_table = ((slots // owned) % owners).astype(bf16)
    owner = jnp.sum(jnp.where(in_low, dot(owner_table, in_high, 0, 0), 0.0), axis=0, keepdims=True).astype(i32)
    at_owner = iota((owners, rows), 0) == owner
    before = (iota((rows, rows), 0) < iota((rows, rows), 1)).astype(bf16)
    earlier = dot(at_owner.astype(bf16), before, 1, 0)
    rank = jnp.sum(jnp.where(at_owner, earlier, 0.0), axis=0, keepdims=True).astype(i32)
    position = owner * cap + rank
    place[...] = position
    block = 256
    for b in range(owners * cap // block):
        pick = (iota((block, rows), 0) + b * block == position).astype(bf16)
        moved = dot(pick, vectors[...], 1, 0).astype(bf16)
        send[b * block // cap : (b + 1) * block // cap] = moved.reshape(block // cap, cap, -1)
    for b in range(book.shape[0] // block):
        at = slice(b * block, (b + 1) * block)
        book_squares[:, at] = as_row(row_squares(book[at]))
    for side, points in enumerate((vectors, vectors2)):
        for b in range(rows // block):
            at = slice(b * block, (b + 1) * block)
            vector_squares[:, side * rows + b * block : side * rows + (b + 1) * block] = as_row(row_squares(points[at]))
    base = where[0]
    cell_index = (iota((high, low), 0) * low + iota((high, low), 1)).astype(f32)
    line = iota((16, 128), 0)
    ids = jnp.full((16, 128), -1.0, f32)
    for first, start in ((0, base), (8, base ^ owned)):
        for s in range(owned):
            hit = jnp.where(slots == start + s, cell_index, 0.0)
            cell_id = jnp.sum(jnp.sum(hit, axis=1, keepdims=True), axis=0, keepdims=True)
            ids = jnp.where(line == first + s, cell_id, ids)
    wanted[...] = ids


def locals_kernel(where, ids, ids2, wanted, local):
    core = where[2]
    places = local.shape[1]
    rows = SETS * 128
    cap = places // (GROUPS * CORES)
    cells = [wanted[s : s + 1, 0:1] for s in range(SETS)]
    before = (iota((rows, rows), 0) < iota((rows, rows), 1)).astype(bf16)
    spread = (iota((cap, places), 1) % cap == iota((cap, places), 0)).astype(bf16)
    at_group = iota((GROUPS, places), 1) // (CORES * cap) == iota((GROUPS, places), 0)
    of_core = (iota((GROUPS, places), 1) // cap) % CORES
    total = jnp.zeros((1, places), f32)
    for source, side in ((ids, core), (ids2, 1 - core)):
        digits = source[...]
        codes = jnp.concatenate([digits[:, j, :] * LOW + digits[:, SETS + j, :] for j in range(SETS)], axis=1)
        found = jnp.zeros(codes.shape, f32)
        for s in range(SETS):
            found = found + jnp.where(codes == cells[s], s + 1.0, 0.0)
        earlier = dot((found > 0.0).astype(bf16), before, 1, 0)
        ranked = jnp.concatenate(
            [jnp.sum(jnp.where(earlier == float(r), found, 0.0), axis=1, keepdims=True) for r in range(cap)], axis=1
        )
        across = dot(ranked.astype(bf16), spread, 1, 0)
        total = total + jnp.sum(jnp.where(at_group & (of_core == side), across, 0.0), axis=0, keepdims=True)
    local[...] = total - 1.0


def coarse_kernel(
    where, vectors, vectors2, vector_squares, wanted, own, right, left, far_a, far_b, early, weights, told, mine, scores
):
    quarter, core = where[1], where[2]
    rows, features = vectors.shape
    cells = wanted[:, 0:1].astype(i32)
    picked = jnp.zeros((16, features), f32)
    tops = [jnp.full((1, rows), -jnp.inf, f32)] * CORES
    half = GROUPS // 2
    for chunk, step, start in zip((own, right, left, far_a, far_b), (0, 1, 3, 2, 2), (0, 0, 0, 0, half), strict=True):
        count = chunk.shape[0] // 8
        at = (quarter + step) % SETS
        points = chunk[...]
        squares = row_squares(points)
        for side, against in enumerate((vectors, vectors2)):
            across = slice(side * rows, (side + 1) * rows)
            distance = vector_squares[:, across] + squares - 2.0 * dot(points, against[...], 1, 1)
            score = -sharpness * distance
            tops[side] = jnp.maximum(tops[side], jnp.max(score, axis=0, keepdims=True))
            scores[start : start + count, at, :, across] = score.reshape(count, 8, rows)
        line = iota((16, count * 8), 1) + start * 8
        inside = (line // 8 * CORES + core) * (SETS * 8) + at * 8 + line % 8 == cells
        picked = picked + dot(inside.astype(bf16), points, 1, 0)
    mine[...] = picked[0:8]
    totals = []
    for side in range(CORES):
        across = slice(side * rows, (side + 1) * rows)
        total = jnp.zeros((1, rows), f32)
        for b in range(GROUPS // 4):
            e = jnp.exp(scores[4 * b : 4 * b + 4, :, :, across].reshape(128, rows) - tops[side])
            total = total + jnp.sum(e, axis=0, keepdims=True)
            weights[4 * b : 4 * b + 4, :, :, across] = e.reshape(4, SETS, 8, rows)
        totals.append(total)
    told[0:8, :] = jnp.broadcast_to(jnp.concatenate(tops, axis=1), (8, CORES * rows))
    told[8:16, :] = jnp.broadcast_to(jnp.concatenate(totals, axis=1), (8, CORES * rows))
    told[16:24, 0:features] = picked[8:16]
    told[16:24, features:] = jnp.zeros((8, CORES * rows - features), f32)


def share_kernel(weights, told, heard, share):
    rows = told.shape[1] // CORES

    def swapped(line):
        return jnp.concatenate([line[:, rows:], line[:, :rows]], axis=1)

    top, total = told[0:1, :], told[8:9, :]
    top2, total2 = swapped(heard[0:1, :]), swapped(heard[8:9, :])
    highest = jnp.maximum(top, top2)
    here = jnp.exp(top - highest)
    factor = here / (total * here + total2 * jnp.exp(top2 - highest))
    for b in range(GROUPS // 4):
        probs = weights[4 * b : 4 * b + 4].reshape(128, CORES * rows) * factor
        lanes = probs[:, 0:128]
        for j in range(1, CORES * rows // 128):
            lanes = lanes + probs[:, j * 128 : (j + 1) * 128]
        share[b : b + 1, :] = jnp.sum(jnp.transpose(lanes), axis=0, keepdims=True)


def fine_kernel(got, local, mine, heard, book, book_squares, spread, out, weights, residual, mass):
    owners, cap = spread.shape
    rows, features = got.shape
    fine = book.shape[0] // SETS
    centres = (mine[...] + heard[16:24, 0:features]).astype(bf16)
    squares = [
        jnp.transpose(jnp.broadcast_to(book_squares[:, s * fine : (s + 1) * fine], (128, fine)))[:, 0:1] for s in range(SETS)
    ]
    block = 256
    parts = []
    for b in range(rows // block):
        at = slice(b * block, (b + 1) * block)
        slot = local[:, at]
        inside = [slot == s for s in range(SETS)]
        chosen = (iota((8, block), 0).astype(f32) == slot).astype(bf16)
        moved = (got[at].astype(f32) - dot(chosen, centres, 0, 0)).astype(bf16)
        residual[at] = moved
        moved_squares = as_row(row_squares(moved))
        distance = jnp.zeros((fine, block), f32)
        for s in range(SETS):
            here = moved_squares + squares[s] - 2.0 * dot(book[s * fine : (s + 1) * fine], moved, 1, 1)
            distance = jnp.where(inside[s], here, distance)
        score = -sharpness * distance
        e = jnp.exp(score - jnp.max(score, axis=0, keepdims=True))
        weight = e * ((slot >= 0.0).astype(f32) / jnp.sum(e, axis=0, keepdims=True))
        parts.append(jnp.sum(weight * distance, axis=0, keepdims=True) / features)
        for s in range(SETS):
            of = slice(s * fine, (s + 1) * fine)
            only = jnp.where(inside[s], weight, 0.0)
            weights[of, at] = only.astype(bf16)
            part = jnp.sum(only, axis=1, keepdims=True)
            mass[of] = part if b == 0 else mass[of] + part
    row = jnp.concatenate(parts, axis=1)
    places = (iota((cap, rows), 1) % cap == iota((cap, rows), 0)).astype(f32)
    at_owner = iota((owners, rows), 1) // cap == iota((owners, rows), 0)
    spread[...] = dot(jnp.where(at_owner, row, 0.0), places, 1, 1, lax.Precision.HIGHEST)
    for s in range(SETS):
        of = slice(s * fine, (s + 1) * fine)
        total = dot(weights[of], residual[...], 1, 0)
        out[of] = ((book[of].astype(f32) + total) * (1.0 / (1.0 + mass[of]))).astype(bf16)


def answer_kernel(where, spread, shares, out):
    owners, cap = spread.shape
    total = jnp.sum(shares[...], axis=0).reshape(X, 2, 128)
    quarter = jnp.sum(jnp.where(iota(total.shape, 0) == where[3], total, 0.0), axis=0)
    line = jnp.concatenate([spread[...], jnp.zeros((owners, 128 - cap), f32)], axis=1)
    out[:, 0:2, :] = jnp.broadcast_to(quarter[None], (owners, 2, 128))
    out[:, 2:4, :] = jnp.broadcast_to(line[:, None, :], (owners, 2, 128))


def finish_kernel(scale, got, place, distortion, share):
    owners = got.shape[0]
    rows = place.shape[1]
    cap = 2 * rows // owners
    position = place[...]
    at_owner = (iota((owners, rows), 0) == position // cap).astype(f32)
    at_rank = iota((cap, rows), 0) == position % cap
    whole = got[...]
    returned = whole[:, 2, :][:, 0:cap]
    across = dot(returned, at_owner, 0, 0, lax.Precision.HIGHEST)
    distortion[...] = jnp.sum(jnp.where(at_rank, across, 0.0), axis=0, keepdims=True)
    quarters = jnp.sum(whole[:, 0:2, :].reshape(Y, X * CORES, 2, 128), axis=0) * scale
    halves = [jnp.concatenate([quarters[x * CORES + c] for x in range(X)], axis=0) for c in range(CORES)]
    for u in range(2):
        pieces = [
            halves[c][:, u * 64 + v * 32 : u * 64 + (v + 1) * 32] for v in range(2) for c in range(CORES)
        ]
        share[:, u, :] = jnp.concatenate(pieces, axis=1)


def exchange(x, axes):
    return lax.all_to_all(x, axes, 0, 0, tiled=True)


def from_next(x, steps):
    return lax.ppermute(x, "z", [((i + steps) % Z, i) for i in range(Z)])


def from_partner(x):
    return lax.ppermute(x, "c", [(0, 1), (1, 0)])


def on_device(vectors, cell_of, cell_slot, coarse, fine_book):
    rows, features = vectors.shape
    owned, fine, _ = fine_book.shape
    owners = GROUPS * CORES
    cap = 2 * rows // owners
    cells = cell_slot.shape[0]
    part = coarse.shape[0] // SETS
    chunk = GROUPS * part
    z, x, c = (lax.axis_index(axis) for axis in ("z", "x", "c"))
    base = lax.axis_index(EVERY) * owned
    where = jnp.stack([base, z % SETS, c, x]).astype(i32)
    book = fine_book.reshape(owned * fine, features)

    packed = call(
        pack_kernel, shaped((GROUPS, part, features + 128), bf16), [where], [coarse, cell_of.reshape(-1, 128)], "pack", 10**6
    )
    first = exchange(packed, ("y", "x"))
    vectors2 = from_partner(vectors)
    send, place, book_squares, vector_squares, wanted = call(
        functools.partial(prepare_kernel, owned),
        (
            shaped((owners, cap, features), bf16),
            shaped((1, rows), i32),
            shaped((1, owned * fine), f32),
            shaped((1, CORES * rows), f32),
            shaped((16, 128), f32),
        ),
        [where],
        [cell_of.reshape(1, rows), cell_slot.reshape(-1, LOW), vectors, vectors2, book],
        "prepare",
        10**9,
    )
    got = exchange(send, PLANE).reshape(owners * cap, features)

    own, own_a, own_b, ids = call(
        split_kernel,
        (
            shaped((chunk, features), bf16),
            shaped((chunk // 2, features), bf16),
            shaped((chunk // 2, features), bf16),
            shaped((GROUPS, part, 128), f32),
        ),
        [],
        [first],
        "split",
        10**6,
    )
    right, left = from_next(own, 1), from_next(own, -1)
    far_a, far_b = from_next(own_a, 2), from_next(own_b, -2)
    ids2 = from_partner(ids)
    local = call(locals_kernel, shaped((1, owners * cap), f32), [where], [ids, ids2, wanted], "locals", 10**9)
    weights, told, mine = call(
        coarse_kernel,
        (
            shaped((GROUPS, SETS, part, CORES * rows), f32),
            shaped((24, CORES * rows), f32),
            shaped((8, features), f32),
        ),
        [where],
        [vectors, vectors2, vector_squares, wanted, own, right, left, far_a, far_b, local],
        "coarse_part",
        2 * 10**9,
        mib=28,
        scratch=[pltpu.VMEM((GROUPS, SETS, part, CORES * rows), f32)],
    )
    heard = from_partner(told)
    share = call(share_kernel, shaped((8, 128), f32), [], [weights, told, heard], "share", 10**9)
    shares = exchange(jnp.broadcast_to(share[None], (Z * X, 8, 128)), ("z", "x"))

    spread, fine_next = call(
        fine_kernel,
        (shaped((owners, cap), f32), shaped(book.shape, bf16)),
        [],
        [got, local, mine, heard, book, book_squares],
        "fine_part",
        6 * 10**9,
        mib=24,
        scratch=[
            pltpu.VMEM((owned * fine, owners * cap), bf16),
            pltpu.VMEM((owners * cap, features), bf16),
            pltpu.VMEM((owned * fine, 1), f32),
        ],
    )
    answer = call(answer_kernel, shaped((owners, 4, 128), f32), [where], [spread, shares], "answer", 10**6)
    back = exchange(answer, PLANE)
    distortion, coarse_share = call(
        functools.partial(finish_kernel, owned / rows),
        (shaped((1, rows), f32), shaped((8, 2, 128), f32)),
        [],
        [back, place],
        "finish",
        10**8,
    )
    return (coarse_share.reshape(cells), fine_next.reshape(fine_book.shape), distortion.reshape(rows))


def solution(mesh):
    grid = Mesh(mesh.devices.reshape(Z, Y, X, CORES), EVERY)
    return jax.shard_map(
        on_device,
        mesh=grid,
        in_specs=(P(EVERY, None), P(EVERY), P(), P(PLANE, None), P(EVERY, None, None)),
        out_specs=(P(), P(EVERY, None, None), P(EVERY)),
        check_vma=False,
    )
```

```python
import functools

import jax
import jax.numpy as jnp
from jax import lax
from jax.experimental import pallas as pl
from jax.experimental.pallas import tpu as pltpu
from jax.sharding import Mesh, PartitionSpec as P

sharpness = 0.0625
Z, Y, X, CORES = 8, 8, 4, 2
PLANE = ("y", "x", "c")
EVERY = ("zh", "zl", "y", "x", "c")
FOUR = ("zl", "c")
GROUPS = Y * X
PAIR = 2
TEAM = PAIR * CORES
SLOTS = 4
LOW = 128
f32, bf16, i32 = jnp.float32, jnp.bfloat16, jnp.int32
VMEM = pl.BlockSpec(memory_space=pltpu.VMEM)
SMEM = pl.BlockSpec(memory_space=pltpu.SMEM)
ANY = pl.BlockSpec(memory_space=pl.ANY)
FAR = pl.BlockSpec(memory_space=pltpu.HBM)


def call(body, out_shape, scalars, arrays, name, flops, mib=16, scratch=(), far_in=(), far_out=(), loose=()):
    specs = [ANY if i in loose else FAR if i in far_in else VMEM for i in range(len(arrays))]
    many = isinstance(out_shape, tuple)
    return pl.pallas_call(
        body,
        out_shape=out_shape,
        in_specs=[SMEM] * len(scalars) + specs,
        out_specs=tuple(FAR if i in far_out else VMEM for i in range(len(out_shape))) if many else FAR if far_out else VMEM,
        scratch_shapes=scratch,
        name=name,
        compiler_params=pltpu.CompilerParams(vmem_limit_bytes=mib * 2**20),
        cost_estimate=pl.CostEstimate(flops=flops, bytes_accessed=2**20, transcendentals=0),
    )(*scalars, *arrays)


def shaped(shape, dtype):
    return jax.ShapeDtypeStruct(shape, dtype)


def iota(shape, axis):
    return lax.broadcasted_iota(i32, shape, axis)


def dot(a, b, ca, cb, precision=None):
    return lax.dot_general(
        a, b, (((ca,), (cb,)), ((), ())), preferred_element_type=f32, precision=precision
    )


def as_row(column):
    return jnp.transpose(jnp.broadcast_to(column, (column.shape[0], 128)))[0:1, :]


def row_squares(points):
    wide = points.astype(f32)
    return jnp.sum(wide * wide, axis=1, keepdims=True)


def pack_kernel(coarse, cell, out, coarse_in, cell_in, line, in_sem, out_sem):
    half, features = coarse_in.shape
    fetches = [
        pltpu.make_async_copy(coarse.at[pl.ds(pl.multiple_of(lax.axis_index("zl") * half, half), half)], coarse_in, in_sem.at[0]),
        pltpu.make_async_copy(cell, cell_in, in_sem.at[1]),
    ]
    for fetch in fetches:
        fetch.start()
    for fetch in fetches:
        fetch.wait()
    digits = [cell_in[...] // LOW, cell_in[...] % LOW]
    ids = jnp.concatenate([*digits, jnp.zeros((half - 2 * cell.shape[0], 128), i32)], axis=0).astype(f32)
    line[:, 0:features] = coarse_in[...]
    line[:, features:] = ids.astype(bf16)
    stores = [pltpu.make_async_copy(line, out.at[y], out_sem.at[y]) for y in range(Y)]
    for store in stores:
        store.start()
    for store in stores:
        store.wait()


def route_kernel(
    owned, cell, table, vectors, book, early, send, place, book_squares, wanted,
    cell_in, table_in, rows_in, book_in, rows_out, in_sem, out_sem,
):
    owners, cap, _ = send.shape
    rows = vectors.shape[0]
    pairs = ((cell, cell_in), (table, table_in), (vectors, rows_in), (book, book_in))
    fetches = [pltpu.make_async_copy(source, target, in_sem.at[i]) for i, (source, target) in enumerate(pairs)]
    for fetch in fetches:
        fetch.start()
    fetches[0].wait()
    fetches[1].wait()
    high, low = table.shape
    cell_of = cell_in[...]
    slots = table_in[...]
    in_high = (iota((high, rows), 0) == cell_of // low).astype(bf16)
    in_low = iota((low, rows), 0) == cell_of % low
    owner_table = ((slots // owned) % owners).astype(bf16)
    owner = jnp.sum(jnp.where(in_low, dot(owner_table, in_high, 0, 0), 0.0), axis=0, keepdims=True).astype(i32)
    at_owner = iota((owners, rows), 0) == owner
    before = (iota((rows, rows), 0) < iota((rows, rows), 1)).astype(bf16)
    earlier = dot(at_owner.astype(bf16), before, 1, 0)
    rank = jnp.sum(jnp.where(at_owner, earlier, 0.0), axis=0, keepdims=True).astype(i32)
    position = owner * cap + rank
    place[...] = position
    fetches[2].wait()
    block = 256
    count = block // cap
    stores = []
    for b in range(owners // count):
        pick = (iota((block, rows), 0) + b * block == position).astype(bf16)
        moved = dot(pick, rows_in[...], 1, 0).astype(bf16)
        rows_out[b * count : (b + 1) * count] = moved.reshape(count, cap, -1)
        at = pl.ds(b * count, count)
        store = pltpu.make_async_copy(rows_out.at[at], send.at[at], out_sem.at[b])
        store.start()
        stores.append(store)
    cell_index = (iota((high, low), 0) * low + iota((high, low), 1)).astype(f32)
    line = iota((TEAM * owned, 128), 0)
    ids = jnp.full(line.shape, -1.0, f32)
    for member in range(TEAM):
        start = (lax.axis_index(EVERY) ^ (member % CORES + member // CORES * GROUPS * CORES)) * owned
        for s in range(owned):
            hit = jnp.where(slots == start + s, cell_index, 0.0)
            cell_id = jnp.sum(jnp.sum(hit, axis=1, keepdims=True), axis=0, keepdims=True)
            ids = jnp.where(line == member * owned + s, cell_id, ids)
    wanted[...] = ids
    fetches[3].wait()
    for b in range(book.shape[0] // block):
        at = slice(b * block, (b + 1) * block)
        book_squares[:, at] = as_row(row_squares(book_in[at]))
    for store in stores:
        store.wait()


def coarse_kernel(
    cap, vectors, vectors2, vectors3, vectors4, wanted, gathered, weights, told, scores
):
    parity, core = lax.axis_index("zl"), lax.axis_index("c")
    rows, features = vectors.shape
    part = scores.shape[2]
    slab = Y * part
    cells = wanted[:, 0:1].astype(i32)
    points = gathered[:, 0:features]
    squares = -sharpness * row_squares(points)
    told[...] = jnp.zeros(told.shape, f32)
    tops = []
    for side, against in enumerate((vectors, vectors2, vectors3, vectors4)):
        across = slice(side * rows, (side + 1) * rows)
        vector_squares = -sharpness * as_row(row_squares(against[...]))
        score = (vector_squares + squares) + (2.0 * sharpness) * dot(points, against[...], 1, 1)
        tops.append(jnp.max(score, axis=0, keepdims=True))
        for x in range(X):
            scores[:, x, :, across] = score[x * slab : (x + 1) * slab].reshape(Y, part, rows)
    line = iota((TEAM * SLOTS, X * slab), 1)
    group = line // part % Y * X + line // slab
    inside = (group * CORES + core) * (PAIR * part) + parity * part + line % part == cells
    told[8:24, :] = dot(inside.astype(bf16), points, 1, 0)
    for side in range(TEAM):
        across = slice(side * rows, (side + 1) * rows)
        total = jnp.zeros((1, rows), f32)
        for y in range(Y):
            e = jnp.exp(scores[y, :, :, across].reshape(X * part, rows) - tops[side])
            total = total + jnp.sum(e, axis=0, keepdims=True)
            weights[y, :, :, across] = e.reshape(X, part, rows)
        told[side : side + 1, 0:rows] = tops[side]
        told[4 + side : 5 + side, 0:rows] = total
    ids = gathered[:, features:].astype(f32).reshape(GROUPS, part, 128)
    codes = jnp.concatenate([ids[:, j, :] * LOW + ids[:, 4 + j, :] for j in range(4)], axis=1)
    places = GROUPS * CORES * cap
    before = (iota((rows, rows), 0) < iota((rows, rows), 1)).astype(bf16)
    spread = (iota((cap, places), 1) % cap == iota((cap, places), 0)).astype(bf16)
    source = iota((GROUPS, places), 0)
    target = iota((GROUPS, places), 1) // cap
    filled = (source % Y * X + source // Y) * CORES + core == target
    for member in range(CORES):
        found = jnp.zeros(codes.shape, f32)
        for s in range(SLOTS):
            at = member * SLOTS + s
            found = found + jnp.where(codes == wanted[at : at + 1, 0:1], s + 1.0, 0.0)
        earlier = dot((found > 0.0).astype(bf16), before, 1, 0)
        ranked = jnp.concatenate(
            [jnp.sum(jnp.where(earlier == float(r), found, 0.0), axis=1, keepdims=True) for r in range(cap)], axis=1
        )
        across = dot(ranked.astype(bf16), spread, 1, 0)
        row = jnp.sum(jnp.where(filled, across, 0.0), axis=0, keepdims=True)
        for half in range(2):
            at = 24 + 2 * member + half
            told[at : at + 1, 0 : places // 2] = row[:, half * places // 2 : (half + 1) * places // 2]


def share_kernel(rows, weights, heard, shares):
    me = lax.axis_index(FOUR)
    factors = []
    for side in range(TEAM):
        tops = [heard[me ^ t, t ^ side : (t ^ side) + 1, 0:rows] for t in range(TEAM)]
        totals = [heard[me ^ t, 4 + (t ^ side) : 5 + (t ^ side), 0:rows] for t in range(TEAM)]
        highest = functools.reduce(jnp.maximum, tops)
        total = sum(n * jnp.exp(top - highest) for n, top in zip(totals, tops, strict=True))
        factors.append(jnp.exp(tops[0] - highest) / total)
    factor = jnp.concatenate(factors, axis=1)
    for b in range(Y // 2):
        probs = weights[2 * b : 2 * b + 2].reshape(128, TEAM * rows) * factor
        lanes = probs[:, 0:128]
        for j in range(1, TEAM * rows // 128):
            lanes = lanes + probs[:, j * 128 : (j + 1) * 128]
        share = jnp.sum(jnp.transpose(lanes), axis=0, keepdims=True)
        shares[:, b : b + 1, :] = jnp.broadcast_to(share[None], (shares.shape[0], 1, 128))


def fine_kernel(
    got, heard, book, book_squares, spread, out, weights, residual
):
    owners, cap = spread.shape
    rows, features = got.shape
    fine = book.shape[0] // SLOTS
    me = lax.axis_index(FOUR)
    centres = sum(heard[me ^ t, 8 + t * SLOTS : 8 + (t + 1) * SLOTS, :] for t in range(TEAM))
    centres = jnp.concatenate([centres, jnp.zeros(centres.shape, f32)], axis=0).astype(bf16)
    halves = [heard[me, 24 + h : 25 + h, 0 : rows // 2] + heard[me ^ 1, 26 + h : 27 + h, 0 : rows // 2] for h in range(2)]
    local = jnp.concatenate(halves, axis=1) - 1.0
    squares = [
        jnp.transpose(jnp.broadcast_to(book_squares[:, s * fine : (s + 1) * fine], (128, fine)))[:, 0:1] for s in range(SLOTS)
    ]
    block = 256
    moved_squares = []
    for b in range(rows // block):
        at = slice(b * block, (b + 1) * block)
        chosen = (iota((8, block), 0).astype(f32) == local[:, at]).astype(bf16)
        moved = (got[at].astype(f32) - dot(chosen, centres, 0, 0)).astype(bf16)
        residual[at] = moved
        moved_squares.append(as_row(row_squares(moved)))
    parts = []
    masses = [jnp.zeros((fine, 1), f32)] * SLOTS
    for b in range(rows // block):
        at = slice(b * block, (b + 1) * block)
        slot = local[:, at]
        inside = [slot == s for s in range(SLOTS)]
        distance = jnp.zeros((fine, block), f32)
        for s in range(SLOTS):
            products = dot(book[s * fine : (s + 1) * fine], residual[at], 1, 1)
            distance = jnp.where(inside[s], moved_squares[b] + squares[s] - 2.0 * products, distance)
        score = -sharpness * distance
        e = jnp.exp(score - jnp.max(score, axis=0, keepdims=True))
        weight = e * ((slot >= 0.0).astype(f32) / jnp.sum(e, axis=0, keepdims=True))
        parts.append(jnp.sum(weight * distance, axis=0, keepdims=True) / features)
        for s in range(SLOTS):
            only = jnp.where(inside[s], weight, 0.0)
            weights[s * fine : (s + 1) * fine, at] = only.astype(bf16)
            masses[s] = masses[s] + jnp.sum(only, axis=1, keepdims=True)
    row = jnp.concatenate(parts, axis=1)
    places = (iota((cap, rows), 1) % cap == iota((cap, rows), 0)).astype(f32)
    at_owner = iota((owners, rows), 1) // cap == iota((owners, rows), 0)
    spread[...] = dot(jnp.where(at_owner, row, 0.0), places, 1, 1, lax.Precision.HIGHEST)
    for s in range(SLOTS):
        at = slice(s * fine, (s + 1) * fine)
        total = dot(weights[at], residual[...], 1, 0)
        out[at] = ((book[at].astype(f32) + total) * (1.0 / (1.0 + masses[s]))).astype(bf16)


def answer_kernel(spread, shares, out):
    owners, cap = spread.shape
    total = jnp.sum(jnp.sum(shares[...].reshape(Z // PAIR, PAIR, X, 4, 128), axis=2), axis=0).reshape(X, 2, 128)
    quarter = jnp.sum(jnp.where(iota(total.shape, 0) == lax.axis_index("x"), total, 0.0), axis=0)
    line = jnp.concatenate([spread[...], jnp.zeros((owners, 128 - cap), f32)], axis=1)
    out[:, 0:2, :] = jnp.broadcast_to(quarter[None], (owners, 2, 128))
    out[:, 2:4, :] = jnp.broadcast_to(line[:, None, :], (owners, 2, 128))


def finish_kernel(scale, got, place, distortion, share):
    owners = got.shape[0]
    rows = place.shape[1]
    cap = 2 * rows // owners
    position = place[...]
    at_owner = (iota((owners, rows), 0) == position // cap).astype(f32)
    at_rank = iota((cap, rows), 0) == position % cap
    whole = got[...]
    returned = whole[:, 2, :][:, 0:cap]
    across = dot(returned, at_owner, 0, 0, lax.Precision.HIGHEST)
    distortion[...] = jnp.sum(jnp.where(at_rank, across, 0.0), axis=0, keepdims=True)
    quarters = jnp.sum(whole[:, 0:2, :].reshape(Y, X * CORES, 2, 128), axis=0) * scale
    halves = [jnp.concatenate([quarters[x * CORES + c] for x in range(X)], axis=0) for c in range(CORES)]
    for yl in range(2):
        for xh in range(2):
            pieces = [
                halves[c][p * 4 : p * 4 + 4, yl * 64 + (2 * xh + xl) * 16 : yl * 64 + (2 * xh + xl + 1) * 16]
                for xl in range(2)
                for c in range(CORES)
                for p in range(PAIR)
            ]
            share[:, 2 * yl + xh, :] = jnp.concatenate(pieces, axis=1)


def after(x, *others):
    return pl.pallas_call(
        lambda *refs: None,
        out_shape=shaped(x.shape, x.dtype),
        in_specs=[ANY] * (1 + len(others)),
        out_specs=ANY,
        input_output_aliases={0: 0},
        name="after",
        compiler_params=pltpu.CompilerParams(vmem_limit_bytes=2**20),
    )(x, *others)


def exchange(x, axes):
    return lax.all_to_all(x, axes, 0, 0, tiled=True)


def from_neighbour(x):
    return lax.ppermute(x, "zl", [(0, 1), (1, 0)])


def from_partner(x):
    return lax.ppermute(x, "c", [(0, 1), (1, 0)])


def on_device(vectors, cell_of, cell_slot, coarse, fine_book):
    rows, features = vectors.shape
    owned, fine, _ = fine_book.shape
    owners = GROUPS * CORES
    cap = 2 * rows // owners
    cells = cell_slot.shape[0]
    part = coarse.shape[0] // PAIR
    book = fine_book.reshape(owned * fine, features)
    table = cell_slot.reshape(-1, LOW)

    packed = call(
        pack_kernel,
        shaped((Y, part, features + 128), bf16),
        [],
        [coarse, cell_of.reshape(-1, 128)],
        "pack",
        10**6,
        mib=60,
        far_in=(0, 1),
        far_out=(0,),
        scratch=[
            pltpu.VMEM((part, features), bf16),
            pltpu.VMEM((rows // 128, 128), i32),
            pltpu.VMEM((part, features + 128), bf16),
            pltpu.SemaphoreType.DMA((2,)),
            pltpu.SemaphoreType.DMA((Y,)),
        ],
    )
    first = exchange(packed, ("y",)).reshape(Y * part, features + 128)
    vectors2 = from_partner(vectors)
    send, place, book_squares, wanted = call(
        functools.partial(route_kernel, owned),
        (
            shaped((owners, cap, features), bf16),
            shaped((1, rows), i32),
            shaped((1, owned * fine), f32),
            shaped((TEAM * owned, 128), f32),
        ),
        [],
        [cell_of.reshape(1, rows), table, vectors, book, vectors2],
        "route",
        10**9,
        mib=60,
        far_in=(0, 1, 2, 3),
        far_out=(0,),
        loose=(4,),
        scratch=[
            pltpu.VMEM((1, rows), i32),
            pltpu.VMEM(table.shape, i32),
            pltpu.VMEM((rows, features), bf16),
            pltpu.VMEM(book.shape, bf16),
            pltpu.VMEM((owners, cap, features), bf16),
            pltpu.SemaphoreType.DMA((4,)),
            pltpu.SemaphoreType.DMA((owners * cap // 256,)),
        ],
    )
    got = exchange(send, PLANE).reshape(owners * cap, features)

    gathered = lax.all_gather(first, "x", axis=0, tiled=True)
    vectors3 = after(from_neighbour(vectors), gathered)
    vectors4 = from_partner(vectors3)
    weights, told = call(
        functools.partial(coarse_kernel, cap),
        (shaped((Y, X, part, TEAM * rows), f32), shaped((32, features), f32)),
        [],
        [vectors, vectors2, vectors3, vectors4, wanted, gathered],
        "coarse_part",
        2 * 10**9,
        mib=28,
        scratch=[pltpu.VMEM((Y, X, part, TEAM * rows), f32)],
    )
    heard = lax.all_gather(told, FOUR, axis=0)
    shares = call(
        functools.partial(share_kernel, rows), shaped((Z * X, 4, 128), f32), [], [weights, heard], "share", 10**9
    )
    shares = exchange(shares, ("zh", "zl", "x"))

    spread, fine_next = call(
        fine_kernel,
        (shaped((owners, cap), f32), shaped(book.shape, bf16)),
        [],
        [got, heard, book, book_squares],
        "fine_part",
        3 * 10**9,
        mib=24,
        scratch=[
            pltpu.VMEM((owned * fine, owners * cap), bf16),
            pltpu.VMEM((owners * cap, features), bf16),
        ],
    )
    answer = call(answer_kernel, shaped((owners, 4, 128), f32), [], [spread, shares], "answer", 10**6)
    back = exchange(answer, PLANE)
    distortion, coarse_share = call(
        functools.partial(finish_kernel, owned / rows),
        (shaped((1, rows), f32), shaped((4, 4, 128), f32)),
        [],
        [back, place],
        "finish",
        10**8,
    )
    return (coarse_share.reshape(cells), fine_next.reshape(fine_book.shape), distortion.reshape(rows))


def solution(mesh):
    grid = Mesh(mesh.devices.reshape(Z // PAIR, PAIR, Y, X, CORES), EVERY)
    return jax.shard_map(
        on_device,
        mesh=grid,
        in_specs=(P(EVERY, None), P(EVERY), P(), P(PLANE, None), P(EVERY, None, None)),
        out_specs=(P(), P(EVERY, None, None), P(EVERY)),
        check_vma=False,
    )
```

```python
import functools

import jax
import jax.numpy as jnp
from jax import lax
from jax.experimental import pallas as pl
from jax.experimental.pallas import tpu as pltpu
from jax.sharding import Mesh, PartitionSpec as P

sharpness = 0.0625
Z, Y, X, CORES = 8, 8, 4, 2
PLANE = ("y", "x", "c")
EVERY = ("zh", "zl", "y", "x", "c")
FOUR = ("zl", "c")
GROUPS = Y * X
PAIR = 2
TEAM = PAIR * CORES
SLOTS = 4
LOW = 128
f32, bf16, i32 = jnp.float32, jnp.bfloat16, jnp.int32
VMEM = pl.BlockSpec(memory_space=pltpu.VMEM)
SMEM = pl.BlockSpec(memory_space=pltpu.SMEM)
ANY = pl.BlockSpec(memory_space=pl.ANY)
FAR = pl.BlockSpec(memory_space=pltpu.HBM)


def call(body, out_shape, scalars, arrays, name, flops, mib=16, scratch=(), far_in=(), far_out=(), loose=()):
    specs = [ANY if i in loose else FAR if i in far_in else VMEM for i in range(len(arrays))]
    many = isinstance(out_shape, tuple)
    return pl.pallas_call(
        body,
        out_shape=out_shape,
        in_specs=[SMEM] * len(scalars) + specs,
        out_specs=tuple(FAR if i in far_out else VMEM for i in range(len(out_shape))) if many else FAR if far_out else VMEM,
        scratch_shapes=scratch,
        name=name,
        compiler_params=pltpu.CompilerParams(vmem_limit_bytes=mib * 2**20),
        cost_estimate=pl.CostEstimate(flops=flops, bytes_accessed=2**20, transcendentals=0),
    )(*scalars, *arrays)


def shaped(shape, dtype):
    return jax.ShapeDtypeStruct(shape, dtype)


def iota(shape, axis):
    return lax.broadcasted_iota(i32, shape, axis)


def dot(a, b, ca, cb, precision=None):
    return lax.dot_general(
        a, b, (((ca,), (cb,)), ((), ())), preferred_element_type=f32, precision=precision
    )


def as_row(column):
    return jnp.transpose(jnp.broadcast_to(column, (column.shape[0], 128)))[0:1, :]


def row_squares(points):
    wide = points.astype(f32)
    return jnp.sum(wide * wide, axis=1, keepdims=True)


def pack_kernel(coarse, cell, out, coarse_in, cell_in, line, in_sem, out_sem):
    half, features = coarse_in.shape
    fetches = [
        pltpu.make_async_copy(coarse.at[pl.ds(pl.multiple_of(lax.axis_index("zl") * half, half), half)], coarse_in, in_sem.at[0]),
        pltpu.make_async_copy(cell, cell_in, in_sem.at[1]),
    ]
    for fetch in fetches:
        fetch.start()
    for fetch in fetches:
        fetch.wait()
    digits = [cell_in[...] // LOW, cell_in[...] % LOW]
    ids = jnp.concatenate([*digits, jnp.zeros((half - 2 * cell.shape[0], 128), i32)], axis=0).astype(f32)
    line[:, 0:features] = coarse_in[...]
    line[:, features:] = ids.astype(bf16)
    stores = [pltpu.make_async_copy(line, out.at[y], out_sem.at[y]) for y in range(Y)]
    for store in stores:
        store.start()
    for store in stores:
        store.wait()


def route_kernel(
    owned, cell, table, vectors, book, early, send, place, book_squares, wanted,
    cell_in, table_in, rows_in, book_in, rows_out, in_sem, out_sem,
):
    owners, cap, _ = send.shape
    rows = vectors.shape[0]
    pairs = ((cell, cell_in), (table, table_in), (vectors, rows_in), (book, book_in))
    fetches = [pltpu.make_async_copy(source, target, in_sem.at[i]) for i, (source, target) in enumerate(pairs)]
    for fetch in fetches:
        fetch.start()
    fetches[0].wait()
    fetches[1].wait()
    high, low = table.shape
    cell_of = cell_in[...]
    slots = table_in[...]
    in_high = (iota((high, rows), 0) == cell_of // low).astype(bf16)
    in_low = iota((low, rows), 0) == cell_of % low
    owner_table = ((slots // owned) % owners).astype(bf16)
    owner = jnp.sum(jnp.where(in_low, dot(owner_table, in_high, 0, 0), 0.0), axis=0, keepdims=True).astype(i32)
    at_owner = iota((owners, rows), 0) == owner
    before = (iota((rows, rows), 0) < iota((rows, rows), 1)).astype(bf16)
    earlier = dot(at_owner.astype(bf16), before, 1, 0)
    rank = jnp.sum(jnp.where(at_owner, earlier, 0.0), axis=0, keepdims=True).astype(i32)
    position = owner * cap + rank
    place[...] = position
    fetches[2].wait()
    block = 256
    count = block // cap
    stores = []
    for b in range(owners // count):
        pick = (iota((block, rows), 0) + b * block == position).astype(bf16)
        moved = dot(pick, rows_in[...], 1, 0).astype(bf16)
        rows_out[b * count : (b + 1) * count] = moved.reshape(count, cap, -1)
        at = pl.ds(b * count, count)
        store = pltpu.make_async_copy(rows_out.at[at], send.at[at], out_sem.at[b])
        store.start()
        stores.append(store)
    cell_index = (iota((high, low), 0) * low + iota((high, low), 1)).astype(f32)
    line = iota((TEAM * owned, 128), 0)
    ids = jnp.full(line.shape, -1.0, f32)
    for member in range(TEAM):
        start = (lax.axis_index(EVERY) ^ (member % CORES + member // CORES * GROUPS * CORES)) * owned
        for s in range(owned):
            hit = jnp.where(slots == start + s, cell_index, 0.0)
            cell_id = jnp.sum(jnp.sum(hit, axis=1, keepdims=True), axis=0, keepdims=True)
            ids = jnp.where(line == member * owned + s, cell_id, ids)
    wanted[...] = ids
    fetches[3].wait()
    for b in range(book.shape[0] // block):
        at = slice(b * block, (b + 1) * block)
        book_squares[:, at] = as_row(row_squares(book_in[at]))
    for store in stores:
        store.wait()


def quarter_weights(points, squares, against, scores, weights, across):
    part, rows = scores.shape[2], against.shape[0]
    slab = Y * part
    vector_squares = -sharpness * as_row(row_squares(against[...]))
    score = (vector_squares + squares) + (2.0 * sharpness) * dot(points, against[...], 1, 1)
    for x in range(X):
        scores[:, x, :, across] = score[x * slab : (x + 1) * slab].reshape(Y, part, rows)
    top = jnp.max(score, axis=0, keepdims=True).astype(bf16).astype(f32)
    total = jnp.zeros((1, rows), f32)
    for y in range(Y):
        e = jnp.exp(scores[y, :, :, across].reshape(X * part, rows) - top)
        total = total + jnp.sum(e, axis=0, keepdims=True)
        weights[y, :, :, across] = e.reshape(X, part, rows)
    return top, total


def note_sums(told, side, top, total):
    rows = top.shape[1]
    upper = total.astype(bf16).astype(f32)
    told[side : side + 1, 0:rows] = top
    told[4 + side : 5 + side, 0:rows] = upper
    told[8 + side : 9 + side, 0:rows] = total - upper


def coarse_kernel(cap, vectors, vectors2, vectors3, wanted, gathered, weights, told, scores):
    parity, core = lax.axis_index("zl"), lax.axis_index("c")
    rows, features = vectors.shape
    part = scores.shape[2]
    slab = Y * part
    cells = wanted[:, 0:1].astype(i32)
    points = gathered[:, 0:features]
    squares = -sharpness * row_squares(points)
    told[...] = jnp.zeros(told.shape, f32)
    for side, against in enumerate((vectors, vectors2, vectors3)):
        across = slice(side * rows, (side + 1) * rows)
        note_sums(told, side, *quarter_weights(points, squares, against, scores, weights, across))
    line = iota((TEAM * SLOTS, X * slab), 1)
    group = line // part % Y * X + line // slab
    inside = (group * CORES + core) * (PAIR * part) + parity * part + line % part == cells
    told[12:28, :] = dot(inside.astype(bf16), points, 1, 0)
    ids = gathered[:, features:].astype(f32).reshape(GROUPS, part, 128)
    codes = jnp.concatenate([ids[:, j, :] * LOW + ids[:, 4 + j, :] for j in range(4)], axis=1)
    places = GROUPS * CORES * cap
    before = (iota((rows, rows), 0) < iota((rows, rows), 1)).astype(bf16)
    spread = (iota((cap, places), 1) % cap == iota((cap, places), 0)).astype(bf16)
    source = iota((GROUPS, places), 0)
    target = iota((GROUPS, places), 1) // cap
    filled = (source % Y * X + source // Y) * CORES + core == target
    for member in range(CORES):
        found = jnp.zeros(codes.shape, f32)
        for s in range(SLOTS):
            at = member * SLOTS + s
            found = found + jnp.where(codes == wanted[at : at + 1, 0:1], s + 1.0, 0.0)
        earlier = dot((found > 0.0).astype(bf16), before, 1, 0)
        ranked = jnp.concatenate(
            [jnp.sum(jnp.where(earlier == float(r), found, 0.0), axis=1, keepdims=True) for r in range(cap)], axis=1
        )
        across = dot(ranked.astype(bf16), spread, 1, 0)
        row = jnp.sum(jnp.where(filled, across, 0.0), axis=0, keepdims=True)
        for half in range(2):
            at = 28 + 2 * member + half
            told[at : at + 1, 0 : places // 2] = row[:, half * places // 2 : (half + 1) * places // 2]


def last_kernel(vectors, gathered, so_far, weights, told, scores, notes):
    features = vectors.shape[1]
    points = gathered[:, 0:features]
    notes[...] = so_far[...]
    across = slice(0, vectors.shape[0])
    top, total = quarter_weights(points, -sharpness * row_squares(points), vectors, scores, weights, across)
    note_sums(notes, TEAM - 1, top, total)
    told[...] = notes[...].astype(bf16)


def share_kernel(rows, weights, weights2, heard, shares):
    me = lax.axis_index(FOUR)
    words = [heard[me ^ t].astype(f32) for t in range(TEAM)]
    factors = []
    for side in range(TEAM):
        at = [t ^ side for t in range(TEAM)]
        tops = [words[t][at[t] : at[t] + 1, 0:rows] for t in range(TEAM)]
        totals = [words[t][4 + at[t] : 5 + at[t], 0:rows] + words[t][8 + at[t] : 9 + at[t], 0:rows] for t in range(TEAM)]
        highest = functools.reduce(jnp.maximum, tops)
        total = sum(n * jnp.exp(top - highest) for n, top in zip(totals, tops, strict=True))
        factors.append(jnp.exp(tops[0] - highest) / total)
    for b in range(Y // 2):
        lanes = jnp.zeros((128, 128), f32)
        for side, factor in enumerate(factors):
            source, first = (weights, side * rows) if side < TEAM - 1 else (weights2, 0)
            probs = source[2 * b : 2 * b + 2, :, :, first : first + rows].reshape(128, rows) * factor
            for j in range(rows // 128):
                lanes = lanes + probs[:, j * 128 : (j + 1) * 128]
        share = jnp.sum(jnp.transpose(lanes), axis=0, keepdims=True)
        shares[:, b : b + 1, :] = jnp.broadcast_to(share[None], (shares.shape[0], 1, 128))


def fine_kernel(
    got, heard, book, book_squares, spread, out, weights, residual
):
    owners, cap = spread.shape
    rows, features = got.shape
    fine = book.shape[0] // SLOTS
    me = lax.axis_index(FOUR)
    words = [heard[me ^ t].astype(f32) for t in range(TEAM)]
    centres = sum(words[t][12 + t * SLOTS : 12 + (t + 1) * SLOTS, :] for t in range(TEAM))
    centres = jnp.concatenate([centres, jnp.zeros(centres.shape, f32)], axis=0).astype(bf16)
    halves = [words[0][28 + h : 29 + h, 0 : rows // 2] + words[1][30 + h : 31 + h, 0 : rows // 2] for h in range(2)]
    local = jnp.concatenate(halves, axis=1) - 1.0
    squares = [
        jnp.transpose(jnp.broadcast_to(book_squares[:, s * fine : (s + 1) * fine], (128, fine)))[:, 0:1] for s in range(SLOTS)
    ]
    block = 256
    moved_squares = []
    for b in range(rows // block):
        at = slice(b * block, (b + 1) * block)
        chosen = (iota((8, block), 0).astype(f32) == local[:, at]).astype(bf16)
        moved = (got[at].astype(f32) - dot(chosen, centres, 0, 0)).astype(bf16)
        residual[at] = moved
        moved_squares.append(as_row(row_squares(moved)))
    parts = []
    masses = [jnp.zeros((fine, 1), f32)] * SLOTS
    for b in range(rows // block):
        at = slice(b * block, (b + 1) * block)
        slot = local[:, at]
        inside = [slot == s for s in range(SLOTS)]
        distance = jnp.zeros((fine, block), f32)
        for s in range(SLOTS):
            products = dot(book[s * fine : (s + 1) * fine], residual[at], 1, 1)
            distance = jnp.where(inside[s], moved_squares[b] + squares[s] - 2.0 * products, distance)
        score = -sharpness * distance
        e = jnp.exp(score - jnp.max(score, axis=0, keepdims=True))
        weight = e * ((slot >= 0.0).astype(f32) / jnp.sum(e, axis=0, keepdims=True))
        parts.append(jnp.sum(weight * distance, axis=0, keepdims=True) / features)
        for s in range(SLOTS):
            only = jnp.where(inside[s], weight, 0.0)
            weights[s * fine : (s + 1) * fine, at] = only.astype(bf16)
            masses[s] = masses[s] + jnp.sum(only, axis=1, keepdims=True)
    row = jnp.concatenate(parts, axis=1)
    places = (iota((cap, rows), 1) % cap == iota((cap, rows), 0)).astype(f32)
    at_owner = iota((owners, rows), 1) // cap == iota((owners, rows), 0)
    spread[...] = dot(jnp.where(at_owner, row, 0.0), places, 1, 1, lax.Precision.HIGHEST)
    for s in range(SLOTS):
        at = slice(s * fine, (s + 1) * fine)
        total = dot(weights[at], residual[...], 1, 0)
        out[at] = ((book[at].astype(f32) + total) * (1.0 / (1.0 + masses[s]))).astype(bf16)


def answer_kernel(spread, shares, out):
    owners, cap = spread.shape
    total = jnp.sum(jnp.sum(shares[...].reshape(Z // PAIR, PAIR, X, 4, 128), axis=2), axis=0).reshape(X, 2, 128)
    quarter = jnp.sum(jnp.where(iota(total.shape, 0) == lax.axis_index("x"), total, 0.0), axis=0)
    upper = spread[...].astype(bf16).astype(f32)
    line = jnp.concatenate([upper, spread[...] - upper, jnp.zeros((owners, 128 - 2 * cap), f32)], axis=1)
    top = jnp.broadcast_to(quarter[None], (owners, 2, 128))
    out[...] = jnp.concatenate([top, jnp.broadcast_to(line[:, None, :], (owners, 2, 128))], axis=1).astype(bf16)


def finish_kernel(scale, got, place, distortion, share):
    owners = got.shape[0]
    rows = place.shape[1]
    cap = 2 * rows // owners
    position = place[...]
    at_owner = (iota((owners, rows), 0) == position // cap).astype(f32)
    at_rank = iota((cap, rows), 0) == position % cap
    whole = got[...].astype(f32)
    line = whole[:, 2, :]
    returned = line[:, 0:cap] + line[:, cap : 2 * cap]
    across = dot(returned, at_owner, 0, 0, lax.Precision.HIGHEST)
    distortion[...] = jnp.sum(jnp.where(at_rank, across, 0.0), axis=0, keepdims=True)
    quarters = jnp.sum(whole[:, 0:2, :].reshape(Y, X * CORES, 2, 128), axis=0) * scale
    halves = [jnp.concatenate([quarters[x * CORES + c] for x in range(X)], axis=0) for c in range(CORES)]
    for yl in range(2):
        for xh in range(2):
            pieces = [
                halves[c][p * 4 : p * 4 + 4, yl * 64 + (2 * xh + xl) * 16 : yl * 64 + (2 * xh + xl + 1) * 16]
                for xl in range(2)
                for c in range(CORES)
                for p in range(PAIR)
            ]
            share[:, 2 * yl + xh, :] = jnp.concatenate(pieces, axis=1)


def after(x, *others):
    return pl.pallas_call(
        lambda *refs: None,
        out_shape=shaped(x.shape, x.dtype),
        in_specs=[ANY] * (1 + len(others)),
        out_specs=ANY,
        input_output_aliases={0: 0},
        name="after",
        compiler_params=pltpu.CompilerParams(vmem_limit_bytes=2**20),
    )(x, *others)


def exchange(x, axes):
    return lax.all_to_all(x, axes, 0, 0, tiled=True)


def from_neighbour(x):
    return lax.ppermute(x, "zl", [(0, 1), (1, 0)])


def from_partner(x):
    return lax.ppermute(x, "c", [(0, 1), (1, 0)])


def on_device(vectors, cell_of, cell_slot, coarse, fine_book):
    rows, features = vectors.shape
    owned, fine, _ = fine_book.shape
    owners = GROUPS * CORES
    cap = 2 * rows // owners
    cells = cell_slot.shape[0]
    part = coarse.shape[0] // PAIR
    book = fine_book.reshape(owned * fine, features)
    table = cell_slot.reshape(-1, LOW)

    packed = call(
        pack_kernel,
        shaped((Y, part, features + 128), bf16),
        [],
        [coarse, cell_of.reshape(-1, 128)],
        "pack",
        10**6,
        mib=60,
        far_in=(0, 1),
        far_out=(0,),
        scratch=[
            pltpu.VMEM((part, features), bf16),
            pltpu.VMEM((rows // 128, 128), i32),
            pltpu.VMEM((part, features + 128), bf16),
            pltpu.SemaphoreType.DMA((2,)),
            pltpu.SemaphoreType.DMA((Y,)),
        ],
    )
    first = exchange(packed, ("y",)).reshape(Y * part, features + 128)
    vectors2 = from_partner(vectors)
    send, place, book_squares, wanted = call(
        functools.partial(route_kernel, owned),
        (
            shaped((owners, cap, features), bf16),
            shaped((1, rows), i32),
            shaped((1, owned * fine), f32),
            shaped((TEAM * owned, 128), f32),
        ),
        [],
        [cell_of.reshape(1, rows), table, vectors, book, vectors2],
        "route",
        10**9,
        mib=60,
        far_in=(0, 1, 2, 3),
        far_out=(0,),
        loose=(4,),
        scratch=[
            pltpu.VMEM((1, rows), i32),
            pltpu.VMEM(table.shape, i32),
            pltpu.VMEM((rows, features), bf16),
            pltpu.VMEM(book.shape, bf16),
            pltpu.VMEM((owners, cap, features), bf16),
            pltpu.SemaphoreType.DMA((4,)),
            pltpu.SemaphoreType.DMA((owners * cap // 256,)),
        ],
    )
    got = exchange(send, PLANE).reshape(owners * cap, features)

    gathered = lax.all_gather(first, "x", axis=0, tiled=True)
    vectors3 = after(from_neighbour(vectors), gathered)
    vectors4 = from_partner(vectors3)
    weights, told = call(
        functools.partial(coarse_kernel, cap),
        (shaped((Y, X, part, (TEAM - 1) * rows), f32), shaped((32, features), f32)),
        [],
        [vectors, vectors2, vectors3, wanted, gathered],
        "coarse_part",
        2 * 10**9,
        mib=28,
        scratch=[pltpu.VMEM((Y, X, part, (TEAM - 1) * rows), f32)],
    )
    weights2, told = call(
        last_kernel,
        (shaped((Y, X, part, rows), f32), shaped((32, features), bf16)),
        [],
        [vectors4, gathered, told],
        "last_part",
        10**9,
        scratch=[pltpu.VMEM((Y, X, part, rows), f32), pltpu.VMEM((32, features), f32)],
    )
    heard = lax.all_gather(told, FOUR, axis=0)
    shares = call(
        functools.partial(share_kernel, rows),
        shaped((Z * X, 4, 128), f32),
        [],
        [weights, weights2, heard],
        "share",
        10**9,
    )
    shares = exchange(shares, ("zh", "zl", "x"))

    spread, fine_next = call(
        fine_kernel,
        (shaped((owners, cap), f32), shaped(book.shape, bf16)),
        [],
        [got, heard, book, book_squares],
        "fine_part",
        3 * 10**9,
        mib=24,
        scratch=[
            pltpu.VMEM((owned * fine, owners * cap), bf16),
            pltpu.VMEM((owners * cap, features), bf16),
        ],
    )
    answer = call(answer_kernel, shaped((owners, 4, 128), bf16), [], [spread, shares], "answer", 10**6)
    back = exchange(answer, PLANE)
    distortion, coarse_share = call(
        functools.partial(finish_kernel, owned / rows),
        (shaped((1, rows), f32), shaped((4, 4, 128), f32)),
        [],
        [back, place],
        "finish",
        10**8,
    )
    return (coarse_share.reshape(cells), fine_next.reshape(fine_book.shape), distortion.reshape(rows))


def solution(mesh):
    grid = Mesh(mesh.devices.reshape(Z // PAIR, PAIR, Y, X, CORES), EVERY)
    return jax.shard_map(
        on_device,
        mesh=grid,
        in_specs=(P(EVERY, None), P(EVERY), P(), P(PLANE, None), P(EVERY, None, None)),
        out_specs=(P(), P(EVERY, None, None), P(EVERY)),
        check_vma=False,
    )
```

```python
import functools

import jax
import jax.numpy as jnp
from jax import lax
from jax.experimental import pallas as pl
from jax.experimental.pallas import tpu as pltpu
from jax.sharding import Mesh, PartitionSpec as P

sharpness = 0.0625
Z, Y, X, CORES = 8, 8, 4, 2
PLANE = ("y", "x", "c")
EVERY = ("zh", "zl", "y", "x", "c")
FOUR = ("zl", "c")
GROUPS = Y * X
PAIR = 2
TEAM = PAIR * CORES
SLOTS = 4
LOW = 128
f32, bf16, i32 = jnp.float32, jnp.bfloat16, jnp.int32
VMEM = pl.BlockSpec(memory_space=pltpu.VMEM)
SMEM = pl.BlockSpec(memory_space=pltpu.SMEM)
ANY = pl.BlockSpec(memory_space=pl.ANY)
FAR = pl.BlockSpec(memory_space=pltpu.HBM)


def call(body, out_shape, scalars, arrays, name, flops, mib=16, scratch=(), far_in=(), far_out=()):
    specs = [FAR if i in far_in else VMEM for i in range(len(arrays))]
    many = isinstance(out_shape, tuple)
    return pl.pallas_call(
        body,
        out_shape=out_shape,
        in_specs=[SMEM] * len(scalars) + specs,
        out_specs=tuple(FAR if i in far_out else VMEM for i in range(len(out_shape))) if many else FAR if far_out else VMEM,
        scratch_shapes=scratch,
        name=name,
        compiler_params=pltpu.CompilerParams(vmem_limit_bytes=mib * 2**20),
        cost_estimate=pl.CostEstimate(flops=flops, bytes_accessed=2**20, transcendentals=0),
    )(*scalars, *arrays)


def shaped(shape, dtype):
    return jax.ShapeDtypeStruct(shape, dtype)


def iota(shape, axis):
    return lax.broadcasted_iota(i32, shape, axis)


def dot(a, b, ca, cb):
    return lax.dot_general(a, b, (((ca,), (cb,)), ((), ())), preferred_element_type=f32)


def as_row(column):
    return jnp.transpose(jnp.broadcast_to(column, (column.shape[0], 128)))[0:1, :]


def row_squares(points):
    wide = points.astype(f32)
    return jnp.sum(wide * wide, axis=1, keepdims=True)


def pack_kernel(coarse, cell, out, coarse_in, cell_in, line, in_sem, out_sem):
    half, features = coarse_in.shape
    fetches = [
        pltpu.make_async_copy(coarse.at[pl.ds(pl.multiple_of(lax.axis_index("zl") * half, half), half)], coarse_in, in_sem.at[0]),
        pltpu.make_async_copy(cell, cell_in, in_sem.at[1]),
    ]
    for fetch in fetches:
        fetch.start()
    for fetch in fetches:
        fetch.wait()
    digits = [cell_in[...] // LOW, cell_in[...] % LOW]
    ids = jnp.concatenate([*digits, jnp.zeros((half - 2 * cell.shape[0], 128), i32)], axis=0).astype(f32)
    line[:, 0:features] = coarse_in[...]
    line[:, features:] = ids.astype(bf16)
    stores = [pltpu.make_async_copy(line, out.at[y], out_sem.at[y]) for y in range(Y)]
    for store in stores:
        store.start()
    for store in stores:
        store.wait()


def route_kernel(
    owned, cell, table, vectors, book, send, place, book_squares, wanted,
    cell_in, table_in, rows_in, book_in, rows_out, in_sem, out_sem,
):
    owners, cap, _ = send.shape
    rows = vectors.shape[0]
    pairs = ((cell, cell_in), (table, table_in), (vectors, rows_in), (book, book_in))
    fetches = [pltpu.make_async_copy(source, target, in_sem.at[i]) for i, (source, target) in enumerate(pairs)]
    for fetch in fetches:
        fetch.start()
    fetches[0].wait()
    fetches[1].wait()
    high, low = table.shape
    cell_of = cell_in[...]
    slots = table_in[...]
    in_high = (iota((high, rows), 0) == cell_of // low).astype(bf16)
    in_low = iota((low, rows), 0) == cell_of % low
    owner_table = ((slots // owned) % owners).astype(bf16)
    owner = jnp.sum(jnp.where(in_low, dot(owner_table, in_high, 0, 0), 0.0), axis=0, keepdims=True).astype(i32)
    at_owner = iota((owners, rows), 0) == owner
    before = (iota((rows, rows), 0) < iota((rows, rows), 1)).astype(bf16)
    earlier = dot(at_owner.astype(bf16), before, 1, 0)
    rank = jnp.sum(jnp.where(at_owner, earlier, 0.0), axis=0, keepdims=True).astype(i32)
    position = owner * cap + rank
    place[...] = position
    fetches[2].wait()
    block = 256
    count = block // cap
    stores = []
    for b in range(owners // count):
        pick = (iota((block, rows), 0) + b * block == position).astype(bf16)
        moved = dot(pick, rows_in[...], 1, 0).astype(bf16)
        rows_out[b * count : (b + 1) * count] = moved.reshape(count, cap, -1)
        at = pl.ds(b * count, count)
        store = pltpu.make_async_copy(rows_out.at[at], send.at[at], out_sem.at[b])
        store.start()
        stores.append(store)
    cell_index = (iota((high, low), 0) * low + iota((high, low), 1)).astype(f32)
    line = iota((TEAM * owned, 128), 0)
    ids = jnp.full(line.shape, -1.0, f32)
    for member in range(TEAM):
        start = (lax.axis_index(EVERY) ^ (member % CORES + member // CORES * GROUPS * CORES)) * owned
        for s in range(owned):
            hit = jnp.where(slots == start + s, cell_index, 0.0)
            cell_id = jnp.sum(jnp.sum(hit, axis=1, keepdims=True), axis=0, keepdims=True)
            ids = jnp.where(line == member * owned + s, cell_id, ids)
    wanted[...] = ids
    fetches[3].wait()
    for b in range(book.shape[0] // block):
        at = slice(b * block, (b + 1) * block)
        book_squares[:, at] = as_row(row_squares(book_in[at]))
    for store in stores:
        store.wait()


def quarter_weights(points, squares, against, scores, weights, across):
    part, rows = scores.shape[2], against.shape[0]
    slab = Y * part
    vector_squares = -sharpness * as_row(row_squares(against[...]))
    score = (vector_squares + squares) + (2.0 * sharpness) * dot(points, against[...], 1, 1)
    for x in range(X):
        scores[:, x, :, across] = score[x * slab : (x + 1) * slab].reshape(Y, part, rows)
    top = jnp.max(score, axis=0, keepdims=True).astype(bf16).astype(f32)
    total = jnp.zeros((1, rows), f32)
    for y in range(Y):
        e = jnp.exp(scores[y, :, :, across].reshape(X * part, rows) - top)
        total = total + jnp.sum(e, axis=0, keepdims=True)
        weights[y, :, :, across] = e.reshape(X, part, rows)
    return top, total


def note_sums(told, side, top, total):
    rows = top.shape[1]
    upper = total.astype(bf16).astype(f32)
    told[side : side + 1, 0:rows] = top
    told[4 + side : 5 + side, 0:rows] = upper
    told[8 + side : 9 + side, 0:rows] = total - upper


def coarse_kernel(cap, vectors, vectors3, wanted, gathered, weights, told, scores):
    parity, core = lax.axis_index("zl"), lax.axis_index("c")
    rows, features = vectors.shape
    part = scores.shape[2]
    slab = Y * part
    cells = wanted[:, 0:1].astype(i32)
    points = gathered[:, 0:features]
    squares = -sharpness * row_squares(points)
    told[...] = jnp.zeros(told.shape, f32)
    for place, (side, against) in enumerate(((0, vectors), (2, vectors3))):
        across = slice(place * rows, (place + 1) * rows)
        note_sums(told, side, *quarter_weights(points, squares, against, scores, weights, across))
    line = iota((TEAM * SLOTS, X * slab), 1)
    group = line // part % Y * X + line // slab
    inside = (group * CORES + core) * (PAIR * part) + parity * part + line % part == cells
    told[12:28, :] = dot(inside.astype(bf16), points, 1, 0)
    ids = gathered[:, features:].astype(f32).reshape(GROUPS, part, 128)
    codes = jnp.concatenate([ids[:, j, :] * LOW + ids[:, 4 + j, :] for j in range(4)], axis=1)
    places = GROUPS * CORES * cap
    before = (iota((rows, rows), 0) < iota((rows, rows), 1)).astype(bf16)
    spread = (iota((cap, places), 1) % cap == iota((cap, places), 0)).astype(bf16)
    source = iota((GROUPS, places), 0)
    target = iota((GROUPS, places), 1) // cap
    filled = (source % Y * X + source // Y) * CORES + core == target
    for member in range(CORES):
        found = jnp.zeros(codes.shape, f32)
        for s in range(SLOTS):
            at = member * SLOTS + s
            found = found + jnp.where(codes == wanted[at : at + 1, 0:1], s + 1.0, 0.0)
        earlier = dot((found > 0.0).astype(bf16), before, 1, 0)
        ranked = jnp.concatenate(
            [jnp.sum(jnp.where(earlier == float(r), found, 0.0), axis=1, keepdims=True) for r in range(cap)], axis=1
        )
        across = dot(ranked.astype(bf16), spread, 1, 0)
        row = jnp.sum(jnp.where(filled, across, 0.0), axis=0, keepdims=True)
        for half in range(2):
            at = 28 + 2 * member + half
            told[at : at + 1, 0 : places // 2] = row[:, half * places // 2 : (half + 1) * places // 2]


def last_kernel(vectors2, vectors4, gathered, so_far, weights, told, scores, notes):
    rows, features = vectors2.shape
    points = gathered[:, 0:features]
    squares = -sharpness * row_squares(points)
    notes[...] = so_far[...]
    for place, (side, against) in enumerate(((1, vectors2), (3, vectors4))):
        across = slice(place * rows, (place + 1) * rows)
        note_sums(notes, side, *quarter_weights(points, squares, against, scores, weights, across))
    told[...] = notes[...].astype(bf16)


def share_kernel(rows, weights, weights2, heard, shares):
    me = lax.axis_index(FOUR)
    words = [heard[me ^ t].astype(f32) for t in range(TEAM)]
    factors = []
    for side in range(TEAM):
        at = [t ^ side for t in range(TEAM)]
        tops = [words[t][at[t] : at[t] + 1, 0:rows] for t in range(TEAM)]
        totals = [words[t][4 + at[t] : 5 + at[t], 0:rows] + words[t][8 + at[t] : 9 + at[t], 0:rows] for t in range(TEAM)]
        highest = functools.reduce(jnp.maximum, tops)
        total = sum(n * jnp.exp(top - highest) for n, top in zip(totals, tops, strict=True))
        factors.append(jnp.exp(tops[0] - highest) / total)
    for b in range(Y // 2):
        lanes = jnp.zeros((128, 128), f32)
        for side, factor in enumerate(factors):
            source, first = (weights2 if side % CORES else weights), side // CORES * rows
            probs = source[2 * b : 2 * b + 2, :, :, first : first + rows].reshape(128, rows) * factor
            for j in range(rows // 128):
                lanes = lanes + probs[:, j * 128 : (j + 1) * 128]
        share = jnp.sum(jnp.transpose(lanes), axis=0, keepdims=True)
        shares[:, b : b + 1, :] = jnp.broadcast_to(share[None], (shares.shape[0], 1, 128))


def fine_kernel(
    got, heard, book, book_squares, spread, out, weights, residual
):
    owners, cap = spread.shape[0], spread.shape[1] // 2
    rows, features = got.shape
    fine = book.shape[0] // SLOTS
    me = lax.axis_index(FOUR)
    words = [heard[me ^ t].astype(f32) for t in range(TEAM)]
    centres = sum(words[t][12 + t * SLOTS : 12 + (t + 1) * SLOTS, :] for t in range(TEAM))
    centres = jnp.concatenate([centres, jnp.zeros(centres.shape, f32)], axis=0).astype(bf16)
    halves = [words[0][28 + h : 29 + h, 0 : rows // 2] + words[1][30 + h : 31 + h, 0 : rows // 2] for h in range(2)]
    local = jnp.concatenate(halves, axis=1) - 1.0
    squares = [
        jnp.transpose(jnp.broadcast_to(book_squares[:, s * fine : (s + 1) * fine], (128, fine)))[:, 0:1] for s in range(SLOTS)
    ]
    block = 256
    moved_squares = []
    for b in range(rows // block):
        at = slice(b * block, (b + 1) * block)
        chosen = (iota((8, block), 0).astype(f32) == local[:, at]).astype(bf16)
        moved = (got[at].astype(f32) - dot(chosen, centres, 0, 0)).astype(bf16)
        residual[at] = moved
        moved_squares.append(as_row(row_squares(moved)))
    parts = []
    masses = [jnp.zeros((fine, 1), f32)] * SLOTS
    for b in range(rows // block):
        at = slice(b * block, (b + 1) * block)
        slot = local[:, at]
        inside = [slot == s for s in range(SLOTS)]
        distance = jnp.zeros((fine, block), f32)
        for s in range(SLOTS):
            products = dot(book[s * fine : (s + 1) * fine], residual[at], 1, 1)
            distance = jnp.where(inside[s], moved_squares[b] + squares[s] - 2.0 * products, distance)
        score = -sharpness * distance
        e = jnp.exp(score - jnp.max(score, axis=0, keepdims=True))
        weight = e * ((slot >= 0.0).astype(f32) / jnp.sum(e, axis=0, keepdims=True))
        parts.append(jnp.sum(weight * distance, axis=0, keepdims=True) / features)
        for s in range(SLOTS):
            only = jnp.where(inside[s], weight, 0.0)
            weights[s * fine : (s + 1) * fine, at] = only.astype(bf16)
            masses[s] = masses[s] + jnp.sum(only, axis=1, keepdims=True)
    row = jnp.concatenate(parts, axis=1)
    places = (iota((cap, rows), 1) % cap == iota((cap, rows), 0)).astype(bf16)
    at_owner = iota((owners, rows), 1) // cap == iota((owners, rows), 0)
    upper = row.astype(bf16).astype(f32)
    for part, values in enumerate((upper, row - upper)):
        spread[:, part * cap : (part + 1) * cap] = dot(jnp.where(at_owner, values, 0.0).astype(bf16), places, 1, 1)
    for s in range(SLOTS):
        at = slice(s * fine, (s + 1) * fine)
        total = dot(weights[at], residual[...], 1, 0)
        out[at] = ((book[at].astype(f32) + total) * (1.0 / (1.0 + masses[s]))).astype(bf16)


def answer_kernel(spread, shares, out):
    owners, width = spread.shape
    total = jnp.sum(jnp.sum(shares[...].reshape(Z // PAIR, PAIR, X, 4, 128), axis=2), axis=0).reshape(X, 2, 128)
    quarter = jnp.sum(jnp.where(iota(total.shape, 0) == lax.axis_index("x"), total, 0.0), axis=0)
    line = jnp.concatenate([spread[...], jnp.zeros((owners, 128 - width), f32)], axis=1)
    top = jnp.broadcast_to(quarter[None], (owners, 2, 128))
    out[...] = jnp.concatenate([top, jnp.broadcast_to(line[:, None, :], (owners, 2, 128))], axis=1).astype(bf16)


def finish_kernel(scale, got, place, distortion, share):
    owners = got.shape[0]
    rows = place.shape[1]
    cap = 2 * rows // owners
    position = place[...]
    at_owner = (iota((owners, rows), 0) == position // cap).astype(bf16)
    at_rank = iota((cap, rows), 0) == position % cap
    whole = got[...].astype(f32)
    line = whole[:, 2, :].astype(bf16)
    across = dot(line[:, 0:cap], at_owner, 0, 0) + dot(line[:, cap : 2 * cap], at_owner, 0, 0)
    distortion[...] = jnp.sum(jnp.where(at_rank, across, 0.0), axis=0, keepdims=True)
    quarters = jnp.sum(whole[:, 0:2, :].reshape(Y, X * CORES, 2, 128), axis=0) * scale
    halves = [jnp.concatenate([quarters[x * CORES + c] for x in range(X)], axis=0) for c in range(CORES)]
    for yl in range(2):
        for xh in range(2):
            pieces = [
                halves[c][p * 4 : p * 4 + 4, yl * 64 + (2 * xh + xl) * 16 : yl * 64 + (2 * xh + xl + 1) * 16]
                for xl in range(2)
                for c in range(CORES)
                for p in range(PAIR)
            ]
            share[:, 2 * yl + xh, :] = jnp.concatenate(pieces, axis=1)


def after(x, *others):
    return pl.pallas_call(
        lambda *refs: None,
        out_shape=shaped(x.shape, x.dtype),
        in_specs=[ANY] * (1 + len(others)),
        out_specs=ANY,
        input_output_aliases={0: 0},
        name="after",
        compiler_params=pltpu.CompilerParams(vmem_limit_bytes=2**20),
    )(x, *others)


def exchange(x, axes):
    return lax.all_to_all(x, axes, 0, 0, tiled=True)


def from_neighbour(x):
    return lax.ppermute(x, "zl", [(0, 1), (1, 0)])


def from_partner(x):
    return lax.ppermute(x, "c", [(0, 1), (1, 0)])


def on_device(vectors, cell_of, cell_slot, coarse, fine_book):
    rows, features = vectors.shape
    owned, fine, _ = fine_book.shape
    owners = GROUPS * CORES
    cap = 2 * rows // owners
    cells = cell_slot.shape[0]
    part = coarse.shape[0] // PAIR
    book = fine_book.reshape(owned * fine, features)
    table = cell_slot.reshape(-1, LOW)

    packed = call(
        pack_kernel,
        shaped((Y, part, features + 128), bf16),
        [],
        [coarse, cell_of.reshape(-1, 128)],
        "pack",
        10**6,
        mib=60,
        far_in=(0, 1),
        far_out=(0,),
        scratch=[
            pltpu.VMEM((part, features), bf16),
            pltpu.VMEM((rows // 128, 128), i32),
            pltpu.VMEM((part, features + 128), bf16),
            pltpu.SemaphoreType.DMA((2,)),
            pltpu.SemaphoreType.DMA((Y,)),
        ],
    )
    first = exchange(packed, ("y",)).reshape(Y * part, features + 128)
    send, place, book_squares, wanted = call(
        functools.partial(route_kernel, owned),
        (
            shaped((owners, cap, features), bf16),
            shaped((1, rows), i32),
            shaped((1, owned * fine), f32),
            shaped((TEAM * owned, 128), f32),
        ),
        [],
        [cell_of.reshape(1, rows), table, vectors, book],
        "route",
        10**9,
        mib=60,
        far_in=(0, 1, 2, 3),
        far_out=(0,),
        scratch=[
            pltpu.VMEM((1, rows), i32),
            pltpu.VMEM(table.shape, i32),
            pltpu.VMEM((rows, features), bf16),
            pltpu.VMEM(book.shape, bf16),
            pltpu.VMEM((owners, cap, features), bf16),
            pltpu.SemaphoreType.DMA((4,)),
            pltpu.SemaphoreType.DMA((owners * cap // 256,)),
        ],
    )
    got = exchange(send, PLANE).reshape(owners * cap, features)

    gathered = lax.all_gather(first, "x", axis=0, tiled=True)
    vectors3 = after(from_neighbour(vectors), gathered)
    vectors2, vectors4 = from_partner(vectors), from_partner(vectors3)
    weights, told = call(
        functools.partial(coarse_kernel, cap),
        (shaped((Y, X, part, PAIR * rows), f32), shaped((32, features), f32)),
        [],
        [vectors, vectors3, wanted, gathered],
        "coarse_part",
        2 * 10**9,
        mib=28,
        scratch=[pltpu.VMEM((Y, X, part, PAIR * rows), f32)],
    )
    weights2, told = call(
        last_kernel,
        (shaped((Y, X, part, PAIR * rows), f32), shaped((32, features), bf16)),
        [],
        [vectors2, vectors4, gathered, told],
        "last_part",
        10**9,
        mib=28,
        scratch=[pltpu.VMEM((Y, X, part, PAIR * rows), f32), pltpu.VMEM((32, features), f32)],
    )
    heard = lax.all_gather(told, FOUR, axis=0)
    shares = call(
        functools.partial(share_kernel, rows),
        shaped((Z * X, 4, 128), f32),
        [],
        [weights, weights2, heard],
        "share",
        10**9,
    )
    shares = exchange(shares, ("zh", "zl", "x"))

    spread, fine_next = call(
        fine_kernel,
        (shaped((owners, 2 * cap), f32), shaped(book.shape, bf16)),
        [],
        [got, heard, book, book_squares],
        "fine_part",
        3 * 10**9,
        mib=24,
        scratch=[
            pltpu.VMEM((owned * fine, owners * cap), bf16),
            pltpu.VMEM((owners * cap, features), bf16),
        ],
    )
    answer = call(answer_kernel, shaped((owners, 4, 128), bf16), [], [spread, shares], "answer", 10**6)
    back = exchange(answer, PLANE)
    distortion, coarse_share = call(
        functools.partial(finish_kernel, owned / rows),
        (shaped((1, rows), f32), shaped((4, 4, 128), f32)),
        [],
        [back, place],
        "finish",
        10**8,
    )
    return (coarse_share.reshape(cells), fine_next.reshape(fine_book.shape), distortion.reshape(rows))


def solution(mesh):
    grid = Mesh(mesh.devices.reshape(Z // PAIR, PAIR, Y, X, CORES), EVERY)
    return jax.shard_map(
        on_device,
        mesh=grid,
        in_specs=(P(EVERY, None), P(EVERY), P(), P(PLANE, None), P(EVERY, None, None)),
        out_specs=(P(), P(EVERY, None, None), P(EVERY)),
        check_vma=False,
    )
```

```python
import functools

import jax
import jax.numpy as jnp
from jax import lax
from jax.experimental import pallas as pl
from jax.experimental.pallas import tpu as pltpu
from jax.sharding import Mesh, PartitionSpec as P

sharpness = 0.0625
Z, Y, X, CORES = 8, 8, 4, 2
PLANE = ("y", "x", "c")
EVERY = ("zh", "zl", "y", "x", "c")
FOUR = ("zl", "c")
GROUPS = Y * X
PAIR = 2
TEAM = PAIR * CORES
SLOTS = 4
LOW = 128
f32, bf16, i32 = jnp.float32, jnp.bfloat16, jnp.int32
VMEM = pl.BlockSpec(memory_space=pltpu.VMEM)
SMEM = pl.BlockSpec(memory_space=pltpu.SMEM)
ANY = pl.BlockSpec(memory_space=pl.ANY)
FAR = pl.BlockSpec(memory_space=pltpu.HBM)


def call(body, out_shape, scalars, arrays, name, flops, mib=16, scratch=(), far_in=(), far_out=()):
    specs = [FAR if i in far_in else VMEM for i in range(len(arrays))]
    many = isinstance(out_shape, tuple)
    return pl.pallas_call(
        body,
        out_shape=out_shape,
        in_specs=[SMEM] * len(scalars) + specs,
        out_specs=tuple(FAR if i in far_out else VMEM for i in range(len(out_shape))) if many else FAR if far_out else VMEM,
        scratch_shapes=scratch,
        name=name,
        compiler_params=pltpu.CompilerParams(vmem_limit_bytes=mib * 2**20),
        cost_estimate=pl.CostEstimate(flops=flops, bytes_accessed=2**20, transcendentals=0),
    )(*scalars, *arrays)


def shaped(shape, dtype):
    return jax.ShapeDtypeStruct(shape, dtype)


def iota(shape, axis):
    return lax.broadcasted_iota(i32, shape, axis)


def dot(a, b, ca, cb):
    return lax.dot_general(a, b, (((ca,), (cb,)), ((), ())), preferred_element_type=f32)


def as_row(column):
    return jnp.transpose(jnp.broadcast_to(column, (column.shape[0], 128)))[0:1, :]


def row_squares(points):
    wide = points.astype(f32)
    return jnp.sum(wide * wide, axis=1, keepdims=True)


def pack_kernel(coarse, cell, out, coarse_in, cell_in, line, in_sem, out_sem):
    half, features = coarse_in.shape
    fetches = [
        pltpu.make_async_copy(coarse.at[pl.ds(pl.multiple_of(lax.axis_index("zl") * half, half), half)], coarse_in, in_sem.at[0]),
        pltpu.make_async_copy(cell, cell_in, in_sem.at[1]),
    ]
    for fetch in fetches:
        fetch.start()
    for fetch in fetches:
        fetch.wait()
    digits = [cell_in[...] // LOW, cell_in[...] % LOW]
    ids = jnp.concatenate([*digits, jnp.zeros((half - 2 * cell.shape[0], 128), i32)], axis=0).astype(f32)
    line[:, 0:features] = coarse_in[...]
    line[:, features:] = ids.astype(bf16)
    stores = [pltpu.make_async_copy(line, out.at[y], out_sem.at[y]) for y in range(Y)]
    for store in stores:
        store.start()
    for store in stores:
        store.wait()


def route_kernel(
    owned, cell, table, vectors, book, send, place, book_squares, wanted,
    cell_in, table_in, rows_in, book_in, rows_out, in_sem, out_sem,
):
    owners, cap, _ = send.shape
    rows = vectors.shape[0]
    pairs = ((cell, cell_in), (table, table_in), (vectors, rows_in), (book, book_in))
    fetches = [pltpu.make_async_copy(source, target, in_sem.at[i]) for i, (source, target) in enumerate(pairs)]
    for fetch in fetches:
        fetch.start()
    fetches[0].wait()
    fetches[1].wait()
    high, low = table.shape
    cell_of = cell_in[...]
    slots = table_in[...]
    in_high = (iota((high, rows), 0) == cell_of // low).astype(bf16)
    in_low = iota((low, rows), 0) == cell_of % low
    owner_table = ((slots // owned) % owners).astype(bf16)
    owner = jnp.sum(jnp.where(in_low, dot(owner_table, in_high, 0, 0), 0.0), axis=0, keepdims=True).astype(i32)
    at_owner = iota((owners, rows), 0) == owner
    before = (iota((rows, rows), 0) < iota((rows, rows), 1)).astype(bf16)
    earlier = dot(at_owner.astype(bf16), before, 1, 0)
    rank = jnp.sum(jnp.where(at_owner, earlier, 0.0), axis=0, keepdims=True).astype(i32)
    position = owner * cap + rank
    place[...] = position
    fetches[2].wait()
    block = 256
    count = block // cap
    stores = []
    for b in range(owners // count):
        pick = (iota((block, rows), 0) + b * block == position).astype(bf16)
        moved = dot(pick, rows_in[...], 1, 0).astype(bf16)
        rows_out[b * count : (b + 1) * count] = moved.reshape(count, cap, -1)
        at = pl.ds(b * count, count)
        store = pltpu.make_async_copy(rows_out.at[at], send.at[at], out_sem.at[b])
        store.start()
        stores.append(store)
    cell_index = (iota((high, low), 0) * low + iota((high, low), 1)).astype(f32)
    line = iota((TEAM * owned, 128), 0)
    ids = jnp.full(line.shape, -1.0, f32)
    for member in range(TEAM):
        start = (lax.axis_index(EVERY) ^ (member % CORES + member // CORES * GROUPS * CORES)) * owned
        for s in range(owned):
            hit = jnp.where(slots == start + s, cell_index, 0.0)
            cell_id = jnp.sum(jnp.sum(hit, axis=1, keepdims=True), axis=0, keepdims=True)
            ids = jnp.where(line == member * owned + s, cell_id, ids)
    wanted[...] = ids
    fetches[3].wait()
    for b in range(book.shape[0] // block):
        at = slice(b * block, (b + 1) * block)
        book_squares[:, at] = as_row(row_squares(book_in[at]))
    for store in stores:
        store.wait()


def quarter_weights(points, squares, against, scores, weights, across):
    part, rows = scores.shape[2], against.shape[0]
    slab = Y * part
    vector_squares = -sharpness * as_row(row_squares(against[...]))
    score = (vector_squares + squares) + (2.0 * sharpness) * dot(points, against[...], 1, 1)
    for x in range(X):
        scores[:, x, :, across] = score[x * slab : (x + 1) * slab].reshape(Y, part, rows)
    top = jnp.max(score, axis=0, keepdims=True).astype(bf16).astype(f32)
    total = jnp.zeros((1, rows), f32)
    for y in range(Y):
        e = jnp.exp(scores[y, :, :, across].reshape(X * part, rows) - top)
        total = total + jnp.sum(e, axis=0, keepdims=True)
        weights[y, :, :, across] = e.reshape(X, part, rows)
    return top, total


def note_sums(told, side, top, total):
    rows = top.shape[1]
    upper = total.astype(bf16).astype(f32)
    told[side : side + 1, 0:rows] = top
    told[4 + side : 5 + side, 0:rows] = upper
    told[8 + side : 9 + side, 0:rows] = total - upper


def coarse_kernel(cap, vectors, vectors3, wanted, gathered, weights, told, scores):
    parity, core = lax.axis_index("zl"), lax.axis_index("c")
    rows, features = vectors.shape
    part = scores.shape[2]
    slab = Y * part
    cells = wanted[:, 0:1].astype(i32)
    points = gathered[:, 0:features]
    squares = -sharpness * row_squares(points)
    told[...] = jnp.zeros(told.shape, f32)
    for place, (side, against) in enumerate(((0, vectors), (2, vectors3))):
        across = slice(place * rows, (place + 1) * rows)
        note_sums(told, side, *quarter_weights(points, squares, against, scores, weights, across))
    line = iota((TEAM * SLOTS, X * slab), 1)
    group = line // part % Y * X + line // slab
    inside = (group * CORES + core) * (PAIR * part) + parity * part + line % part == cells
    told[12:28, :] = dot(inside.astype(bf16), points, 1, 0)
    ids = gathered[:, features:].astype(f32).reshape(GROUPS, part, 128)
    codes = jnp.concatenate([ids[:, j, :] * LOW + ids[:, 4 + j, :] for j in range(4)], axis=1)
    places = GROUPS * CORES * cap
    before = (iota((rows, rows), 0) < iota((rows, rows), 1)).astype(bf16)
    spread = (iota((cap, places), 1) % cap == iota((cap, places), 0)).astype(bf16)
    source = iota((GROUPS, places), 0)
    target = iota((GROUPS, places), 1) // cap
    filled = (source % Y * X + source // Y) * CORES + core == target
    for member in range(CORES):
        found = jnp.zeros(codes.shape, f32)
        for s in range(SLOTS):
            at = member * SLOTS + s
            found = found + jnp.where(codes == wanted[at : at + 1, 0:1], s + 1.0, 0.0)
        earlier = dot((found > 0.0).astype(bf16), before, 1, 0)
        ranked = jnp.concatenate(
            [jnp.sum(jnp.where(earlier == float(r), found, 0.0), axis=1, keepdims=True) for r in range(cap)], axis=1
        )
        across = dot(ranked.astype(bf16), spread, 1, 0)
        row = jnp.sum(jnp.where(filled, across, 0.0), axis=0, keepdims=True)
        for half in range(2):
            at = 28 + 2 * member + half
            told[at : at + 1, 0 : places // 2] = row[:, half * places // 2 : (half + 1) * places // 2]


def last_kernel(vectors2, vectors4, gathered, so_far, weights, told, scores, notes):
    rows, features = vectors2.shape
    points = gathered[:, 0:features]
    squares = -sharpness * row_squares(points)
    notes[...] = so_far[...]
    for place, (side, against) in enumerate(((1, vectors2), (3, vectors4))):
        across = slice(place * rows, (place + 1) * rows)
        note_sums(notes, side, *quarter_weights(points, squares, against, scores, weights, across))
    told[...] = notes[...].astype(bf16)


def share_kernel(rows, weights, weights2, heard, shares):
    me = lax.axis_index(FOUR)
    words = [heard[me ^ t].astype(f32) for t in range(TEAM)]
    factors = []
    for side in range(TEAM):
        at = [t ^ side for t in range(TEAM)]
        tops = [words[t][at[t] : at[t] + 1, 0:rows] for t in range(TEAM)]
        totals = [words[t][4 + at[t] : 5 + at[t], 0:rows] + words[t][8 + at[t] : 9 + at[t], 0:rows] for t in range(TEAM)]
        highest = functools.reduce(jnp.maximum, tops)
        total = sum(n * jnp.exp(top - highest) for n, top in zip(totals, tops, strict=True))
        factors.append(jnp.exp(tops[0] - highest) / total)
    lines = []
    for b in range(Y // 2):
        lanes = jnp.zeros((128, 128), f32)
        for side, factor in enumerate(factors):
            source, first = (weights2 if side % CORES else weights), side // CORES * rows
            probs = source[2 * b : 2 * b + 2, :, :, first : first + rows].reshape(128, rows) * factor
            for j in range(rows // 128):
                lanes = lanes + probs[:, j * 128 : (j + 1) * 128]
        lines.append(jnp.sum(jnp.transpose(lanes), axis=0, keepdims=True))
    shares[...] = jnp.broadcast_to(jnp.concatenate(lines, axis=0)[None], shares.shape).astype(bf16)


def fine_kernel(
    got, heard, book, book_squares, spread, out, weights, residual
):
    owners, cap = spread.shape[0], spread.shape[1] // 2
    rows, features = got.shape
    fine = book.shape[0] // SLOTS
    me = lax.axis_index(FOUR)
    words = [heard[me ^ t].astype(f32) for t in range(TEAM)]
    centres = sum(words[t][12 + t * SLOTS : 12 + (t + 1) * SLOTS, :] for t in range(TEAM))
    centres = jnp.concatenate([centres, jnp.zeros(centres.shape, f32)], axis=0).astype(bf16)
    halves = [words[0][28 + h : 29 + h, 0 : rows // 2] + words[1][30 + h : 31 + h, 0 : rows // 2] for h in range(2)]
    local = jnp.concatenate(halves, axis=1) - 1.0
    squares = [
        jnp.transpose(jnp.broadcast_to(book_squares[:, s * fine : (s + 1) * fine], (128, fine)))[:, 0:1] for s in range(SLOTS)
    ]
    block = 256
    moved_squares = []
    for b in range(rows // block):
        at = slice(b * block, (b + 1) * block)
        chosen = (iota((8, block), 0).astype(f32) == local[:, at]).astype(bf16)
        moved = (got[at].astype(f32) - dot(chosen, centres, 0, 0)).astype(bf16)
        residual[at] = moved
        moved_squares.append(as_row(row_squares(moved)))
    parts = []
    masses = [jnp.zeros((fine, 128), f32)] * SLOTS
    for b in range(rows // block):
        at = slice(b * block, (b + 1) * block)
        slot = local[:, at]
        inside = [slot == s for s in range(SLOTS)]
        distance = squares[0] - 2.0 * dot(book[0:fine], residual[at], 1, 1)
        for s in range(1, SLOTS):
            here = squares[s] - 2.0 * dot(book[s * fine : (s + 1) * fine], residual[at], 1, 1)
            distance = jnp.where(inside[s], here, distance)
        distance = moved_squares[b] + distance
        score = -sharpness * distance
        e = jnp.exp(score - jnp.max(score, axis=0, keepdims=True))
        weight = e * ((slot >= 0.0).astype(f32) / jnp.sum(e, axis=0, keepdims=True))
        parts.append(jnp.sum(weight * distance, axis=0, keepdims=True) / features)
        for s in range(SLOTS):
            only = jnp.where(inside[s], weight, 0.0)
            weights[s * fine : (s + 1) * fine, at] = only.astype(bf16)
            masses[s] = masses[s] + only[:, :128] + only[:, 128:]
    masses = [jnp.sum(lanes, axis=1, keepdims=True) for lanes in masses]
    row = jnp.concatenate(parts, axis=1)
    places = (iota((cap, rows), 1) % cap == iota((cap, rows), 0)).astype(bf16)
    at_owner = iota((owners, rows), 1) // cap == iota((owners, rows), 0)
    upper = row.astype(bf16).astype(f32)
    for part, values in enumerate((upper, row - upper)):
        spread[:, part * cap : (part + 1) * cap] = dot(jnp.where(at_owner, values, 0.0).astype(bf16), places, 1, 1)
    for s in range(SLOTS):
        at = slice(s * fine, (s + 1) * fine)
        total = dot(weights[at], residual[...], 1, 0)
        out[at] = ((book[at].astype(f32) + total) * (1.0 / (1.0 + masses[s]))).astype(bf16)


def answer_kernel(spread, shares, out):
    owners, width = spread.shape
    total = jnp.sum(jnp.sum(shares[...].astype(f32).reshape(Z // PAIR, PAIR, X, 4, 128), axis=2), axis=0).reshape(X, 2, 128)
    quarter = jnp.sum(jnp.where(iota(total.shape, 0) == lax.axis_index("x"), total, 0.0), axis=0)
    line = jnp.concatenate([spread[...], jnp.zeros((owners, 128 - width), f32)], axis=1)
    top = jnp.broadcast_to(quarter[None], (owners, 2, 128))
    out[...] = jnp.concatenate([top, jnp.broadcast_to(line[:, None, :], (owners, 2, 128))], axis=1).astype(bf16)


def finish_kernel(scale, got, place, distortion, share):
    owners = got.shape[0]
    rows = place.shape[1]
    cap = 2 * rows // owners
    position = place[...]
    at_owner = (iota((owners, rows), 0) == position // cap).astype(bf16)
    at_rank = iota((cap, rows), 0) == position % cap
    whole = got[...].astype(f32)
    line = whole[:, 2, :].astype(bf16)
    across = dot(line[:, 0:cap], at_owner, 0, 0) + dot(line[:, cap : 2 * cap], at_owner, 0, 0)
    distortion[...] = jnp.sum(jnp.where(at_rank, across, 0.0), axis=0, keepdims=True)
    quarters = jnp.sum(whole[:, 0:2, :].reshape(Y, X * CORES, 2, 128), axis=0) * scale
    halves = [jnp.concatenate([quarters[x * CORES + c] for x in range(X)], axis=0) for c in range(CORES)]
    for yl in range(2):
        for xh in range(2):
            pieces = [
                halves[c][p * 4 : p * 4 + 4, yl * 64 + (2 * xh + xl) * 16 : yl * 64 + (2 * xh + xl + 1) * 16]
                for xl in range(2)
                for c in range(CORES)
                for p in range(PAIR)
            ]
            share[:, 2 * yl + xh, :] = jnp.concatenate(pieces, axis=1)


def after(x, *others):
    return pl.pallas_call(
        lambda *refs: None,
        out_shape=shaped(x.shape, x.dtype),
        in_specs=[ANY] * (1 + len(others)),
        out_specs=ANY,
        input_output_aliases={0: 0},
        name="after",
        compiler_params=pltpu.CompilerParams(vmem_limit_bytes=2**20),
    )(x, *others)


def exchange(x, axes):
    return lax.all_to_all(x, axes, 0, 0, tiled=True)


def from_neighbour(x):
    return lax.ppermute(x, "zl", [(0, 1), (1, 0)])


def from_partner(x):
    return lax.ppermute(x, "c", [(0, 1), (1, 0)])


def on_device(vectors, cell_of, cell_slot, coarse, fine_book):
    rows, features = vectors.shape
    owned, fine, _ = fine_book.shape
    owners = GROUPS * CORES
    cap = 2 * rows // owners
    cells = cell_slot.shape[0]
    part = coarse.shape[0] // PAIR
    book = fine_book.reshape(owned * fine, features)
    table = cell_slot.reshape(-1, LOW)

    packed = call(
        pack_kernel,
        shaped((Y, part, features + 128), bf16),
        [],
        [coarse, cell_of.reshape(-1, 128)],
        "pack",
        10**6,
        mib=60,
        far_in=(0, 1),
        far_out=(0,),
        scratch=[
            pltpu.VMEM((part, features), bf16),
            pltpu.VMEM((rows // 128, 128), i32),
            pltpu.VMEM((part, features + 128), bf16),
            pltpu.SemaphoreType.DMA((2,)),
            pltpu.SemaphoreType.DMA((Y,)),
        ],
    )
    first = exchange(packed, ("y",)).reshape(Y * part, features + 128)
    send, place, book_squares, wanted = call(
        functools.partial(route_kernel, owned),
        (
            shaped((owners, cap, features), bf16),
            shaped((1, rows), i32),
            shaped((1, owned * fine), f32),
            shaped((TEAM * owned, 128), f32),
        ),
        [],
        [cell_of.reshape(1, rows), table, vectors, book],
        "route",
        10**9,
        mib=60,
        far_in=(0, 1, 2, 3),
        far_out=(0,),
        scratch=[
            pltpu.VMEM((1, rows), i32),
            pltpu.VMEM(table.shape, i32),
            pltpu.VMEM((rows, features), bf16),
            pltpu.VMEM(book.shape, bf16),
            pltpu.VMEM((owners, cap, features), bf16),
            pltpu.SemaphoreType.DMA((4,)),
            pltpu.SemaphoreType.DMA((owners * cap // 256,)),
        ],
    )
    got = exchange(send, PLANE).reshape(owners * cap, features)

    gathered = lax.all_gather(first, "x", axis=0, tiled=True)
    vectors3 = after(from_neighbour(vectors), gathered)
    vectors2, vectors4 = from_partner(vectors), from_partner(vectors3)
    weights, told = call(
        functools.partial(coarse_kernel, cap),
        (shaped((Y, X, part, PAIR * rows), f32), shaped((32, features), f32)),
        [],
        [vectors, vectors3, wanted, gathered],
        "coarse_part",
        2 * 10**9,
        mib=28,
        scratch=[pltpu.VMEM((Y, X, part, PAIR * rows), f32)],
    )
    weights2, told = call(
        last_kernel,
        (shaped((Y, X, part, PAIR * rows), f32), shaped((32, features), bf16)),
        [],
        [vectors2, vectors4, gathered, told],
        "last_part",
        10**9,
        mib=28,
        scratch=[pltpu.VMEM((Y, X, part, PAIR * rows), f32), pltpu.VMEM((32, features), f32)],
    )
    heard = lax.all_gather(told, FOUR, axis=0)
    shares = call(
        functools.partial(share_kernel, rows),
        shaped((Z * X, 4, 128), bf16),
        [],
        [weights, weights2, heard],
        "share",
        10**9,
    )
    shares = exchange(shares, ("zh", "zl", "x"))

    spread, fine_next = call(
        fine_kernel,
        (shaped((owners, 2 * cap), f32), shaped(book.shape, bf16)),
        [],
        [got, heard, book, book_squares],
        "fine_part",
        3 * 10**9,
        mib=24,
        scratch=[
            pltpu.VMEM((owned * fine, owners * cap), bf16),
            pltpu.VMEM((owners * cap, features), bf16),
        ],
    )
    answer = call(answer_kernel, shaped((owners, 4, 128), bf16), [], [spread, shares], "answer", 10**6)
    back = exchange(answer, PLANE)
    distortion, coarse_share = call(
        functools.partial(finish_kernel, owned / rows),
        (shaped((1, rows), f32), shaped((4, 4, 128), f32)),
        [],
        [back, place],
        "finish",
        10**8,
    )
    return (coarse_share.reshape(cells), fine_next.reshape(fine_book.shape), distortion.reshape(rows))


def solution(mesh):
    grid = Mesh(mesh.devices.reshape(Z // PAIR, PAIR, Y, X, CORES), EVERY)
    return jax.shard_map(
        on_device,
        mesh=grid,
        in_specs=(P(EVERY, None), P(EVERY), P(), P(PLANE, None), P(EVERY, None, None)),
        out_specs=(P(), P(EVERY, None, None), P(EVERY)),
        check_vma=False,
    )
```
